32 devices in a mesh: round: 8 (over z, y), mp: 4 (over x, core).
Axes of the slice: x: 2, y: 2, z: 4, core: 2. Of those that a mesh axis runs over, the one named last changes fastest.
Arguments:
- tokens: bfloat16 [8, 32, 512], P('round'), may hold values from -8 to 8
- cell_order: int32 [32], replicated, may hold values from 0 to 31, each once
- seam_rows: int32 [8, 8, 2], P('round'), may hold values from -1 to 31, as said below
- obs_mask: int32 [16, 32], replicated, may hold values from 0 to 1, as said below
- norm_gain: float32 [512], replicated, may hold values from 0.1 to 1.9
- w_query: bfloat16 [512, 512], P(None, 'mp'), may hold values from -1 to 1
- w_key: bfloat16 [512, 512], P(None, 'mp'), may hold values from -1 to 1
- w_value: bfloat16 [512, 512], P(None, 'mp'), may hold values from -0.25 to 0.25
- w_out: bfloat16 [512, 512], P('mp'), may hold values from -0.25 to 0.25
- w_gate: bfloat16 [512, 2048], P(None, 'mp'), may hold values from -0.25 to 0.25
- w_up: bfloat16 [512, 2048], P(None, 'mp'), may hold values from -0.25 to 0.25
- w_down: bfloat16 [2048, 512], P('mp'), may hold values from -0.125 to 0.125
- w_read: float32 [512], replicated, may hold values from -0.25 to 0.25
Outputs:
- tiles_out: bfloat16 [8, 32, 512], P('mp', 'round')
- obs_logits: float32 [16], replicated
The draws below stay inside these ranges and needn't reach their ends.
Inputs may be any that keep to these rules, and one draw needn't show every extreme that they name: `seam_rows`: each entry is a row of the sending tile or -1 for an empty slot; the live entries of one tile are all different; a tile's slots to itself are full, and some owner's slots are full from every tile. `obs_mask`: every observable's support holds at least one cell.
All inputs are finite; a program needn't handle non-finite values.
Results may differ from the reference program's by a relative error of at most 0.0052.
The reference program's roundings to bfloat16 on the way (of `permuted`, `normed`, `seam_attn`, `combined` and `hidden`) count: a program that leaves them out, or rounds other values in their place, can miss the bound.
Values may be sent and summed in bfloat16 or wider, within the bound.
No kernel may reach another device: no remote copies, remote signals or barrier semaphores. Data moves between devices by JAX's collectives and lax.ppermute only.
A program may use at most 64 MiB of HBM per device.

```python
import math
import jax
import jax.numpy as jnp
from jax import lax

D = 512
HEADS = 8
HDIM = 64
FF = 2048
OBS = 16
CAP = 2
CELL_DEV = 4
ROUNDS = 8
OWNERS = 8
CELLS = 32
TILE_ROWS = 32


def draw_tokens(key, part):
    shape_all = (ROUNDS, CELLS, D)
    drawn = jnp.clip(jax.random.normal(jax.random.fold_in(key, 1), shape_all, jnp.float32), -6.0, 6.0)
    return drawn.astype(jnp.bfloat16)


def projection(key, salt):
    base = jax.random.normal(jax.random.fold_in(key, salt), (D, D), jnp.float32) / math.sqrt(D)
    base = jnp.clip(base, -0.5, 0.5)
    return base.astype(jnp.bfloat16)


def draw_w_query(key, part):
    return projection(key, 21)


def draw_w_key(key, part):
    return projection(key, 22)


def draw_seam_rows(key, part):
    light_load = jax.random.randint(jax.random.fold_in(key, 31), (OWNERS, OWNERS), 0, CAP + 1)
    heavy_owner = jax.random.randint(jax.random.fold_in(key, 32), (OWNERS,), 0, 8) == 0
    hottest = jax.random.randint(jax.random.fold_in(key, 33), (), 0, OWNERS)
    owners_list = jnp.arange(OWNERS, dtype=jnp.int32)
    filled = heavy_owner[None, :] | (owners_list[None, :] == hottest) | (owners_list[None, :] == owners_list[:, None])
    counts = jnp.where(filled, CAP, light_load)

    def sender_rows(sender):
        shuffled = jax.random.permutation(jax.random.fold_in(jax.random.fold_in(key, 34), sender), TILE_ROWS).astype(jnp.int32)
        where_top = jnp.argmax(shuffled == TILE_ROWS - 1)
        anchor = sender * CAP
        moved_value = shuffled[anchor]
        shuffled = shuffled.at[where_top].set(moved_value).at[anchor].set(TILE_ROWS - 1)
        return shuffled[:OWNERS * CAP].reshape(OWNERS, CAP)
    picked_rows = jax.vmap(sender_rows)(owners_list)
    slot_index = jnp.arange(CAP, dtype=jnp.int32)
    return jnp.where(slot_index[None, None, :] < counts[:, :, None], picked_rows, -1).astype(jnp.int32)


def draw_obs_mask(key, part):
    level = jax.random.randint(jax.random.fold_in(key, 41), (OBS, 1), 8, 33)
    rolls = jax.random.randint(jax.random.fold_in(key, 42), (OBS, CELLS), 0, 64)
    anchor = jax.random.randint(jax.random.fold_in(key, 43), (OBS, 1), 0, CELLS)
    cell_index = jnp.arange(CELLS, dtype=jnp.int32)[None, :]
    return ((rolls < level) | (cell_index == anchor)).astype(jnp.int32)


def block_levels(key, extent, shards, least, high):
    loudness, own = 1.0, jax.random.fold_in(key, 6)
    for position, parts in shards:
        steps = jnp.exp(jax.random.uniform(jax.random.fold_in(own, position), (parts,), jnp.float32, least / len(shards), high / len(shards)))
        loudness = loudness * jnp.repeat(steps, extent[position] // parts).reshape([-1 if axis == position else 1 for axis in range(len(extent))])
    return loudness


def scatter_about(rng, dims, width, limit, cuts=(), held_as=jnp.bfloat16):
    loudness = block_levels(rng, dims, cuts, -0.22, 0.18) if cuts else 1.0
    values = jax.random.normal(rng, dims, jnp.float32) * width * loudness
    return jnp.minimum(jnp.maximum(values, -limit), limit).astype(held_as)


def setup_inputs(seed: int = 0) -> dict:
    arg_keys = jax.random.split(jax.random.key(seed), 14)
    tokens = draw_tokens(jax.random.fold_in(arg_keys[13], 71), 0)
    cell_order = jax.random.permutation(arg_keys[1], CELLS).astype(jnp.int32)
    seam_rows = draw_seam_rows(jax.random.fold_in(arg_keys[13], 71), 0)
    obs_mask = draw_obs_mask(jax.random.fold_in(arg_keys[13], 71), 0)
    norm_gain = jnp.clip(1.0 + 0.18 * jax.random.normal(arg_keys[4], (D,), jnp.float32), 0.1, 1.9)
    w_query = draw_w_query(jax.random.fold_in(arg_keys[13], 71), 0)
    w_key = draw_w_key(jax.random.fold_in(arg_keys[13], 71), 0)
    w_value = scatter_about(arg_keys[7], (D, D), D ** -0.5, 0.25, ((1, 4),))
    w_out = scatter_about(arg_keys[8], (D, D), D ** -0.5, 0.25, ((0, 4),))
    w_gate = scatter_about(arg_keys[9], (D, FF), D ** -0.5, 0.25, ((1, 4),))
    w_up = scatter_about(arg_keys[10], (D, FF), D ** -0.5, 0.25, ((1, 4),))
    w_down = scatter_about(arg_keys[11], (FF, D), FF ** -0.5, 0.125, ((0, 4),))
    w_read = scatter_about(arg_keys[12], (D,), D ** -0.5, 0.25, (), jnp.float32)
    return dict(tokens=tokens, cell_order=cell_order, seam_rows=seam_rows, obs_mask=obs_mask, norm_gain=norm_gain, w_query=w_query, w_key=w_key, w_value=w_value, w_out=w_out, w_gate=w_gate, w_up=w_up, w_down=w_down, w_read=w_read)


norm_eps = 1e-06

def normalize(rows_in, norm_gain):
    values = rows_in.astype(jnp.float32)
    spread = lax.optimization_barrier(jnp.mean(values * values, axis=-1, keepdims=True))
    return (values * lax.rsqrt(spread + norm_eps) * norm_gain).astype(jnp.bfloat16)

def attend(queries, keys_all, values_all, live_keys):
    scale_factor = 1.0 / math.sqrt(queries.shape[-1])
    scores = jnp.einsum('qhe,khe->hqk', queries.astype(jnp.float32), keys_all.astype(jnp.float32)) * scale_factor
    if live_keys is not None:
        scores = jnp.where(live_keys[None, None, :], scores, -1e+30)
    row_max = lax.optimization_barrier(jnp.max(scores, axis=-1, keepdims=True))
    weights = jnp.exp(scores - row_max)
    probabilities = (weights / lax.optimization_barrier(jnp.sum(weights, axis=-1, keepdims=True))).astype(jnp.bfloat16)
    mixture = jnp.einsum('hqk,khe->qhe', probabilities.astype(jnp.float32), values_all.astype(jnp.float32))
    return mixture.reshape(mixture.shape[0], -1)

def reference(tokens, cell_order, seam_rows, obs_mask, norm_gain, w_query, w_key, w_value, w_out, w_gate, w_up, w_down, w_read):
    permuted = tokens[:, cell_order, :]
    tile_tokens = permuted.reshape(ROUNDS, OWNERS, CELL_DEV, D).transpose(1, 0, 2, 3).reshape(OWNERS, TILE_ROWS, D)

    def to_heads(matrix):
        return matrix.reshape(matrix.shape[0], HEADS, HDIM)

    def project(tile_in):
        normed = normalize(tile_in, norm_gain)
        queries = jnp.dot(normed, w_query, preferred_element_type=jnp.float32).astype(jnp.bfloat16)
        keys_all = jnp.dot(normed, w_key, preferred_element_type=jnp.float32).astype(jnp.bfloat16)
        values_all = jnp.dot(normed, w_value, preferred_element_type=jnp.float32).astype(jnp.bfloat16)
        local_attn = attend(to_heads(queries), to_heads(keys_all), to_heads(values_all), None)
        return (normed, queries, keys_all, values_all, local_attn)
    normed, queries, keys_all, values_all, local_attn = lax.map(project, tile_tokens)
    live_slot = seam_rows >= 0
    safe_rows = jnp.where(live_slot, seam_rows, 0).astype(jnp.int32)
    senders = jnp.arange(OWNERS, dtype=jnp.int32)[:, None]

    def owner_attend(owner_index):
        picked = lax.dynamic_index_in_dim(safe_rows, owner_index, 1, keepdims=False)
        live_owner = lax.dynamic_index_in_dim(live_slot, owner_index, 1, keepdims=False).reshape(-1)
        gathered = [source[senders, picked].reshape(OWNERS * CAP, HEADS, HDIM) for source in (queries, keys_all, values_all)]
        return attend(gathered[0], gathered[1], gathered[2], live_owner).astype(jnp.bfloat16)
    seam_attn = lax.map(owner_attend, jnp.arange(OWNERS, dtype=jnp.int32))
    returned = seam_attn.reshape(OWNERS, OWNERS, CAP, D).transpose(1, 0, 2, 3).reshape(OWNERS, OWNERS * CAP, D)
    target = jnp.where(live_slot, seam_rows, TILE_ROWS).astype(jnp.int32).reshape(OWNERS, OWNERS * CAP)
    combined = local_attn.at[senders, target].add(returned.astype(jnp.float32), mode='drop').astype(jnp.bfloat16)

    def finish(pieces):
        tile_in, normed_in, combined_in = pieces
        attn_part = jnp.dot(combined_in, w_out, preferred_element_type=jnp.float32)
        gate_part = jnp.dot(normed_in, w_gate, preferred_element_type=jnp.float32)
        up_part = jnp.dot(normed_in, w_up, preferred_element_type=jnp.float32)
        hidden = (jax.nn.silu(gate_part) * up_part).astype(jnp.bfloat16)
        update = attn_part + jnp.dot(hidden, w_down, preferred_element_type=jnp.float32)
        return (tile_in.astype(jnp.float32) + update).astype(jnp.bfloat16)
    tiles_done = lax.map(finish, (tile_tokens, normed, combined))
    layout = tiles_done.reshape(OWNERS, ROUNDS, CELL_DEV, D).transpose(1, 0, 2, 3).reshape(ROUNDS, CELLS, D)
    support = obs_mask[:, cell_order].astype(jnp.float32)
    pooled = jnp.einsum('oc,rcd->od', support, layout.astype(jnp.float32), precision=lax.Precision.HIGHEST)
    support_count = ROUNDS * lax.optimization_barrier(jnp.sum(obs_mask.astype(jnp.float32), axis=1))
    obs_logits = jnp.dot(pooled, w_read, precision=lax.Precision.HIGHEST) / jnp.sqrt(support_count)
    return (layout, obs_logits)
```

```python
import functools
import math

import jax
import jax.numpy as jnp
from jax import lax
from jax.experimental import pallas as pl
from jax.experimental.pallas import tpu as pltpu
from jax.sharding import PartitionSpec as P

HDIM = 64
SEAM_PAD = 16
VMEM_LIMIT = 32 * 1024 * 1024


norm_eps = 1e-06


def normalize(rows_in, norm_gain):
    values = rows_in.astype(jnp.float32)
    spread = jnp.mean(values * values, axis=-1, keepdims=True)
    return (values * lax.rsqrt(spread + norm_eps) * norm_gain).astype(jnp.bfloat16)


def attend(queries, keys_all, values_all, live_keys):
    scale_factor = 1.0 / math.sqrt(queries.shape[-1])
    scores = (
        jnp.einsum("qhe,khe->hqk", queries, keys_all, preferred_element_type=jnp.float32)
        * scale_factor
    )
    if live_keys is not None:
        scores = jnp.where(live_keys[None, None, :], scores, -1e30)
    row_max = jnp.max(scores, axis=-1, keepdims=True)
    weights = jnp.exp(scores - row_max)
    probabilities = (weights / jnp.sum(weights, axis=-1, keepdims=True)).astype(jnp.bfloat16)
    mixture = jnp.einsum(
        "hqk,khe->qhe", probabilities, values_all, preferred_element_type=jnp.float32
    )
    return mixture.reshape(mixture.shape[0], -1)


def shards_by_tile(
    tokens,
    cell_order,
    seam_rows,
    obs_mask,
    norm_gain,
    w_query,
    w_key,
    w_value,
    w_out,
    w_gate,
    w_up,
    w_down,
    w_read,
):
    round_count = lax.axis_size("round")
    model_count = lax.axis_size("mp")
    model_index = lax.axis_index("mp")
    round_index = lax.axis_index("round")
    width = tokens.shape[2]
    cell_dev = tokens.shape[1] // round_count
    permuted = tokens[:, cell_order, :]
    tile_tokens = lax.all_to_all(permuted, "round", split_axis=1, concat_axis=0, tiled=True)
    tile_rows = tile_tokens.shape[0] * cell_dev
    flat_tokens = tile_tokens.reshape(tile_rows, width)
    normed = normalize(flat_tokens, norm_gain)
    queries = jnp.dot(normed, w_query, preferred_element_type=jnp.float32).astype(jnp.bfloat16)
    keys_all = jnp.dot(normed, w_key, preferred_element_type=jnp.float32).astype(jnp.bfloat16)
    values_all = jnp.dot(normed, w_value, preferred_element_type=jnp.float32).astype(jnp.bfloat16)
    head_width = queries.shape[1]
    heads_dev = head_width // HDIM
    block_rows = min(512, tile_rows)
    query_blocks = queries.reshape(tile_rows // block_rows, block_rows, heads_dev, HDIM)
    key_heads = keys_all.reshape(tile_rows, heads_dev, HDIM)
    value_heads = values_all.reshape(tile_rows, heads_dev, HDIM)
    local_attn = lax.map(
        lambda query_block: attend(query_block, key_heads, value_heads, None), query_blocks
    )
    local_attn = local_attn.reshape(tile_rows, head_width)
    live_slot = seam_rows[0] >= 0
    safe_rows = jnp.where(live_slot, seam_rows[0], 0)
    packet = (
        lax.all_to_all(queries[safe_rows], "round", split_axis=0, concat_axis=0, tiled=True),
        lax.all_to_all(keys_all[safe_rows], "round", split_axis=0, concat_axis=0, tiled=True),
        lax.all_to_all(values_all[safe_rows], "round", split_axis=0, concat_axis=0, tiled=True),
        lax.all_to_all(
            live_slot.astype(jnp.bfloat16), "round", split_axis=0, concat_axis=0, tiled=True
        ),
    )
    seam_queries = packet[0].reshape(-1, heads_dev, HDIM)
    seam_keys = packet[1].reshape(-1, heads_dev, HDIM)
    seam_values = packet[2].reshape(-1, heads_dev, HDIM)
    seam_live = packet[3].reshape(-1) > 0.5
    seam_attn = attend(seam_queries, seam_keys, seam_values, seam_live).astype(jnp.bfloat16)
    returned = lax.all_to_all(
        seam_attn.reshape(round_count, -1, head_width),
        "round",
        split_axis=0,
        concat_axis=0,
        tiled=True,
    )
    target = jnp.where(live_slot, seam_rows[0], tile_rows).reshape(-1)
    combined = (
        local_attn.at[target]
        .add(returned.reshape(-1, head_width).astype(jnp.float32), mode="drop")
        .astype(jnp.bfloat16)
    )
    share_rows = tile_rows // model_count
    own_first = model_index * share_rows
    gate_part = jnp.dot(normed, w_gate, preferred_element_type=jnp.float32)
    up_part = jnp.dot(normed, w_up, preferred_element_type=jnp.float32)
    hidden = (jax.nn.silu(gate_part) * up_part).astype(jnp.bfloat16)
    attn_part = jnp.dot(combined, w_out, preferred_element_type=jnp.float32)
    summed = lax.psum_scatter(
        attn_part + jnp.dot(hidden, w_down, preferred_element_type=jnp.float32),
        "mp",
        scatter_dimension=0,
        tiled=True,
    )
    own_rows = lax.dynamic_slice_in_dim(flat_tokens, own_first, share_rows, 0)
    result_rows = (own_rows.astype(jnp.float32) + summed).astype(jnp.bfloat16)
    tiles_out = result_rows.reshape(share_rows // cell_dev, cell_dev, width)
    my_cells = lax.dynamic_slice_in_dim(cell_order, round_index * cell_dev, cell_dev)
    support = obs_mask[:, my_cells].astype(jnp.float32)
    partial_sum = jnp.einsum(
        "oc,rcd->od", support, tiles_out.astype(jnp.float32), precision=lax.Precision.HIGHEST
    )
    support_count = round_count * jnp.sum(obs_mask.astype(jnp.float32), axis=1)
    divisor = jnp.sqrt(support_count)
    pooled = lax.psum(partial_sum, ("round", "mp"))
    obs_logits = jnp.dot(pooled, w_read, precision=lax.Precision.HIGHEST) / divisor
    return (tiles_out, obs_logits)


def iota(shape, dimension):
    return lax.broadcasted_iota(jnp.int32, shape, dimension)


def one_hot(condition):
    return jnp.where(condition, 1.0, 0.0).astype(jnp.bfloat16)


def dot(left, right):
    return jnp.dot(left, right, preferred_element_type=jnp.float32)


def dot_t(left, right):
    return lax.dot_general(
        left, right, (((1,), (1,)), ((), ())), preferred_element_type=jnp.float32
    )


def split_three(values):
    high = values.astype(jnp.bfloat16)
    rest = values - high.astype(jnp.float32)
    middle = rest.astype(jnp.bfloat16)
    low = (rest - middle.astype(jnp.float32)).astype(jnp.bfloat16)
    return jnp.concatenate([high, middle, low], axis=0)


def softmax(scores):
    weights = jnp.exp(scores - jnp.max(scores, axis=-1, keepdims=True))
    return (weights / jnp.sum(weights, axis=-1, keepdims=True)).astype(jnp.bfloat16)


def layer_kernel(rounds, cells, slots, *refs):
    place, blocks, rest = refs[0], refs[1 : 1 + slots], refs[1 + slots :]
    order, mask_in, gain, w_query, w_key, w_value, w_out, w_gate, w_up, w_down, w_read = rest[:11]
    send, keep, hidden_all, combined_all, tokens_all = rest[11:]
    me, model, core = place[0], place[1], place[2]
    tiles = rounds
    cell_dev = cells // tiles
    tile_rows = rounds * cell_dev
    total = rounds * cells
    width = gain.shape[1]
    head_width = w_query.shape[1]
    observables = mask_in.shape[0]

    def slot_round(slot):
        return me ^ slot ^ jnp.where(slot >= 2, core, 0)

    row = iota((total, 1), 0)
    tile = lax.div(row, tile_rows)
    row_in_tile = lax.rem(row, tile_rows)
    place_in_order = tile * cell_dev + lax.rem(row_in_tile, cell_dev)
    cell = jnp.sum(
        jnp.where(iota((total, cells), 1) == place_in_order, order[...], 0), axis=1, keepdims=True
    )
    source = lax.div(row_in_tile, cell_dev) * cells + cell
    column = iota((1, total), 1)
    held = slot_round(lax.div(column, cells)) * cells + lax.rem(column, cells)
    arrived = jnp.concatenate([block[0, :cells] for block in blocks], axis=0)
    tokens = dot(one_hot(source == held), arrived).astype(jnp.bfloat16)
    tokens_all[...] = tokens

    slots_all = 2 * tiles
    entries = jnp.concatenate([block[0, cells : cells + 1, :slots_all] for block in blocks], axis=0)
    tile_of_slot = slot_round(iota((1, slots), 1))
    seam_entries = dot(one_hot(tile == tile_of_slot), entries)
    matched = seam_entries == row_in_tile.astype(jnp.float32)
    matched_bf = one_hot(matched)
    same_owner = one_hot(
        lax.div(iota((slots_all, slots_all), 0), 2) == lax.div(iota((slots_all, slots_all), 1), 2)
    )
    seam_mask = dot_t(dot(matched_bf, same_owner).astype(jnp.bfloat16), matched_bf) > 0.5
    in_seam = jnp.sum(jnp.where(matched, 1.0, 0.0), axis=1, keepdims=True) > 0.5
    tile_mask = tile == lax.div(column, tile_rows)

    values = tokens.astype(jnp.float32)
    spread = jnp.mean(values * values, axis=-1, keepdims=True)
    normed = (values * lax.rsqrt(spread + norm_eps) * gain[...]).astype(jnp.bfloat16)
    queries = dot(normed, w_query[...]).astype(jnp.bfloat16)
    keys = dot(normed, w_key[...]).astype(jnp.bfloat16)
    vals = dot(normed, w_value[...]).astype(jnp.bfloat16)
    scale = 1.0 / math.sqrt(HDIM)
    lane_head = lax.div(iota((1, head_width), 1), HDIM)
    local = jnp.zeros((total, head_width), jnp.float32)
    seam = jnp.zeros((total, head_width), jnp.float32)
    for head in range(head_width // HDIM):
        mine = lane_head == head
        scores = dot_t(queries, jnp.where(mine, keys, jnp.zeros_like(keys))) * scale
        head_vals = jnp.where(mine, vals, jnp.zeros_like(vals))
        local = local + dot(softmax(jnp.where(tile_mask, scores, -1e30)), head_vals)
        seam = seam + dot(softmax(jnp.where(seam_mask, scores, -1e30)), head_vals)
    seam = seam.astype(jnp.bfloat16).astype(jnp.float32)
    combined = (local + jnp.where(in_seam, seam, 0.0)).astype(jnp.bfloat16)
    combined_all[...] = combined

    gate = dot(normed, w_gate[...])
    up = dot(normed, w_up[...])
    hidden = (gate / (1.0 + jnp.exp(-gate)) * up).astype(jnp.bfloat16)
    hidden_all[...] = hidden

    mask_bf = mask_in[...].astype(jnp.float32).astype(jnp.bfloat16)
    support = dot_t(mask_bf, one_hot(iota((total, cells), 1) == cell)).astype(jnp.bfloat16)
    own = pl.ds(pl.multiple_of(me * tile_rows, tile_rows), tile_rows)
    hidden_rows = jnp.concatenate([hidden_all[own, :], split_three(dot(support, hidden))], axis=0)
    combined_rows = jnp.concatenate(
        [combined_all[own, :], split_three(dot(support, combined))], axis=0
    )
    product = dot(hidden_rows, w_down[...]) + dot(combined_rows, w_out[...])
    first, second, third = (tile_rows + observables * k for k in range(3))
    pooled = (
        product[first : first + observables]
        + product[second : second + observables]
        + product[third : third + observables]
        + jnp.where(model == 0, dot(support, tokens), 0.0)
    )
    count = rounds * jnp.sum(mask_in[...].astype(jnp.float32), axis=1, keepdims=True)
    logits = jnp.sum(pooled * w_read[...], axis=1, keepdims=True) / jnp.sqrt(count)
    diagonal = iota((observables, width), 0) == iota((observables, width), 1)
    logits_row = jnp.sum(jnp.where(diagonal, logits, 0.0), axis=0, keepdims=True)
    logits_tile = jnp.broadcast_to(logits_row, (8, width))

    pairs = send.shape[0]
    share = tile_rows // 4
    update = product[:tile_rows]
    own_tokens = tokens_all[own, :].astype(jnp.float32)
    update = update + jnp.where(lax.div(iota((tile_rows, 1), 0), share) == model, own_tokens, 0.0)
    pair = lax.shift_right_logical(model, 1)
    chunks = [update[share * k : share * (k + 1)] for k in range(4)]

    def chunk(pair_index, core_index):
        low = jnp.where(core_index == 0, chunks[0], chunks[1])
        high = jnp.where(core_index == 0, chunks[2], chunks[3])
        return jnp.where(pair_index == 0, low, high)

    for target, core_index in ((send, 1 - core), (keep, core)):
        target[:share] = chunk(1 - pair, core_index)
        target[share : share + 8] = logits_tile
        target[share + 8 :] = chunk(pair, core_index)


def finish_kernel(share, own, arrived, tiles_out, logits_out):
    cell_dev = tiles_out.shape[1]
    rows = own[8 : 8 + share] + arrived[:share]
    for k in range(tiles_out.shape[0]):
        tiles_out[k] = rows[k * cell_dev : (k + 1) * cell_dev].astype(tiles_out.dtype)
    logits = own[:1] + arrived[share : share + 1]
    logits_out[...] = logits[:, : logits_out.shape[1]]


def shards_whole(
    tokens,
    cell_order,
    seam_rows,
    obs_mask,
    norm_gain,
    w_query,
    w_key,
    w_value,
    w_out,
    w_gate,
    w_up,
    w_down,
    w_read,
):
    rounds = lax.axis_size("round")
    models = lax.axis_size("mp")
    me = lax.axis_index("round")
    model = lax.axis_index("mp")
    cells, width = tokens.shape[1:]
    cell_dev = cells // rounds
    tile_rows = rounds * cell_dev
    share = tile_rows // models
    core = model & 1

    seam_block = jnp.pad(
        seam_rows.reshape(1, 1, -1).astype(jnp.bfloat16),
        ((0, 0), (0, SEAM_PAD - 1), (0, width - seam_rows.size)),
    )
    block = jnp.concatenate([tokens, seam_block], axis=1)

    def fetch(even_step, odd_step):
        pairs = [
            (r * models + m, (r ^ (odd_step if m & 1 else even_step)) * models + m)
            for r in range(rounds)
            for m in range(models)
        ]
        return lax.ppermute(block, ("round", "mp"), pairs)

    def other_core(array):
        return lax.ppermute(array, "mp", [(m, m ^ 1) for m in range(models)])

    direct = {k: fetch(k, k + 1) for k in range(rounds - 2, 0, -2)}
    next_door = fetch(1, 1)
    blocks = [block, next_door]
    for k in range(2, rounds, 2):
        blocks += [direct[k], other_core(direct[k])]

    place = jnp.stack([me, model, core]).astype(jnp.int32)
    vmem = pl.BlockSpec(memory_space=pltpu.VMEM)
    smem = pl.BlockSpec(memory_space=pltpu.SMEM)
    total = rounds * cells
    part = jax.ShapeDtypeStruct((2 * share + 8, width), jnp.float32)
    send, keep = pl.pallas_call(
        functools.partial(layer_kernel, rounds, cells, len(blocks)),
        out_shape=(part, part),
        in_specs=[smem] + [vmem] * (len(blocks) + 11),
        out_specs=(vmem, vmem),
        scratch_shapes=[
            pltpu.VMEM((total, w_gate.shape[1]), jnp.bfloat16),
            pltpu.VMEM((total, w_query.shape[1]), jnp.bfloat16),
            pltpu.VMEM((total, width), jnp.bfloat16),
        ],
        compiler_params=pltpu.CompilerParams(vmem_limit_bytes=VMEM_LIMIT),
    )(
        place,
        *blocks,
        cell_order.reshape(1, -1),
        obs_mask,
        norm_gain.reshape(1, -1),
        w_query,
        w_key,
        w_value,
        w_out,
        w_gate,
        w_up,
        w_down,
        w_read.reshape(1, -1),
    )
    chip = keep + other_core(send)
    arrived = lax.ppermute(chip[: share + 8], "mp", [(m, m ^ 2) for m in range(models)])
    tiles_out, logits = pl.pallas_call(
        functools.partial(finish_kernel, share),
        out_shape=(
            jax.ShapeDtypeStruct((share // cell_dev, cell_dev, width), jnp.bfloat16),
            jax.ShapeDtypeStruct((1, obs_mask.shape[0]), jnp.float32),
        ),
        in_specs=[vmem, vmem],
        out_specs=(vmem, vmem),
    )(chip[share:], arrived)
    return tiles_out, logits.reshape(-1)


def fits_whole(mesh, tokens, seam_rows, w_query):
    rounds, models = mesh.shape["round"], mesh.shape["mp"]
    total = tokens.shape[0] * tokens.shape[1]
    share = total // rounds // models
    return (
        models == 4
        and rounds == tokens.shape[0]
        and rounds & (rounds - 1) == 0
        and rounds > 2
        and total <= 512
        and total // rounds <= 256
        and share % 8 == 0
        and tokens.shape[1] % 16 == 0
        and seam_rows.shape[2] == 2
        and w_query.shape[1] // models % HDIM == 0
    )


def solution(mesh):
    def layer(*args):
        tokens, seam_rows, w_query = args[0], args[2], args[5]
        whole = fits_whole(mesh, tokens, seam_rows, w_query)
        return placed(mesh, shards_whole if whole else shards_by_tile)(*args)

    return layer


def placed(mesh, shards):
    return jax.shard_map(
        shards,
        mesh=mesh,
        in_specs=(
            P("round", None, None),
            P(),
            P("round", None, None),
            P(),
            P(),
            P(None, "mp"),
            P(None, "mp"),
            P(None, "mp"),
            P("mp", None),
            P(None, "mp"),
            P(None, "mp"),
            P("mp", None),
            P(),
        ),
        out_specs=(P("mp", "round", None), P()),
        check_vma=False,
    )
```

```python
import functools
import math

import jax
import jax.numpy as jnp
from jax import lax
from jax.experimental import pallas as pl
from jax.experimental.pallas import tpu as pltpu
from jax.sharding import PartitionSpec as P

HDIM = 64
SEAM_PAD = 16
LANES = 128
SMALL_LIMIT = 8 * 1024 * 1024
LAYER_LIMIT = 32 * 1024 * 1024


norm_eps = 1e-06


def normalize(rows_in, norm_gain):
    values = rows_in.astype(jnp.float32)
    spread = jnp.mean(values * values, axis=-1, keepdims=True)
    return (values * lax.rsqrt(spread + norm_eps) * norm_gain).astype(jnp.bfloat16)


def attend(queries, keys_all, values_all, live_keys):
    scale_factor = 1.0 / math.sqrt(queries.shape[-1])
    scores = (
        jnp.einsum("qhe,khe->hqk", queries, keys_all, preferred_element_type=jnp.float32)
        * scale_factor
    )
    if live_keys is not None:
        scores = jnp.where(live_keys[None, None, :], scores, -1e30)
    row_max = jnp.max(scores, axis=-1, keepdims=True)
    weights = jnp.exp(scores - row_max)
    probabilities = (weights / jnp.sum(weights, axis=-1, keepdims=True)).astype(jnp.bfloat16)
    mixture = jnp.einsum(
        "hqk,khe->qhe", probabilities, values_all, preferred_element_type=jnp.float32
    )
    return mixture.reshape(mixture.shape[0], -1)


def shards_by_tile(
    tokens,
    cell_order,
    seam_rows,
    obs_mask,
    norm_gain,
    w_query,
    w_key,
    w_value,
    w_out,
    w_gate,
    w_up,
    w_down,
    w_read,
):
    round_count = lax.axis_size("round")
    model_count = lax.axis_size("mp")
    model_index = lax.axis_index("mp")
    round_index = lax.axis_index("round")
    width = tokens.shape[2]
    cell_dev = tokens.shape[1] // round_count
    permuted = tokens[:, cell_order, :]
    tile_tokens = lax.all_to_all(permuted, "round", split_axis=1, concat_axis=0, tiled=True)
    tile_rows = tile_tokens.shape[0] * cell_dev
    flat_tokens = tile_tokens.reshape(tile_rows, width)
    normed = normalize(flat_tokens, norm_gain)
    queries = jnp.dot(normed, w_query, preferred_element_type=jnp.float32).astype(jnp.bfloat16)
    keys_all = jnp.dot(normed, w_key, preferred_element_type=jnp.float32).astype(jnp.bfloat16)
    values_all = jnp.dot(normed, w_value, preferred_element_type=jnp.float32).astype(jnp.bfloat16)
    head_width = queries.shape[1]
    heads_dev = head_width // HDIM
    block_rows = min(512, tile_rows)
    query_blocks = queries.reshape(tile_rows // block_rows, block_rows, heads_dev, HDIM)
    key_heads = keys_all.reshape(tile_rows, heads_dev, HDIM)
    value_heads = values_all.reshape(tile_rows, heads_dev, HDIM)
    local_attn = lax.map(
        lambda query_block: attend(query_block, key_heads, value_heads, None), query_blocks
    )
    local_attn = local_attn.reshape(tile_rows, head_width)
    live_slot = seam_rows[0] >= 0
    safe_rows = jnp.where(live_slot, seam_rows[0], 0)
    packet = (
        lax.all_to_all(queries[safe_rows], "round", split_axis=0, concat_axis=0, tiled=True),
        lax.all_to_all(keys_all[safe_rows], "round", split_axis=0, concat_axis=0, tiled=True),
        lax.all_to_all(values_all[safe_rows], "round", split_axis=0, concat_axis=0, tiled=True),
        lax.all_to_all(
            live_slot.astype(jnp.bfloat16), "round", split_axis=0, concat_axis=0, tiled=True
        ),
    )
    seam_queries = packet[0].reshape(-1, heads_dev, HDIM)
    seam_keys = packet[1].reshape(-1, heads_dev, HDIM)
    seam_values = packet[2].reshape(-1, heads_dev, HDIM)
    seam_live = packet[3].reshape(-1) > 0.5
    seam_attn = attend(seam_queries, seam_keys, seam_values, seam_live).astype(jnp.bfloat16)
    returned = lax.all_to_all(
        seam_attn.reshape(round_count, -1, head_width),
        "round",
        split_axis=0,
        concat_axis=0,
        tiled=True,
    )
    target = jnp.where(live_slot, seam_rows[0], tile_rows).reshape(-1)
    combined = (
        local_attn.at[target]
        .add(returned.reshape(-1, head_width).astype(jnp.float32), mode="drop")
        .astype(jnp.bfloat16)
    )
    share_rows = tile_rows // model_count
    own_first = model_index * share_rows
    gate_part = jnp.dot(normed, w_gate, preferred_element_type=jnp.float32)
    up_part = jnp.dot(normed, w_up, preferred_element_type=jnp.float32)
    hidden = (jax.nn.silu(gate_part) * up_part).astype(jnp.bfloat16)
    attn_part = jnp.dot(combined, w_out, preferred_element_type=jnp.float32)
    summed = lax.psum_scatter(
        attn_part + jnp.dot(hidden, w_down, preferred_element_type=jnp.float32),
        "mp",
        scatter_dimension=0,
        tiled=True,
    )
    own_rows = lax.dynamic_slice_in_dim(flat_tokens, own_first, share_rows, 0)
    result_rows = (own_rows.astype(jnp.float32) + summed).astype(jnp.bfloat16)
    tiles_out = result_rows.reshape(share_rows // cell_dev, cell_dev, width)
    my_cells = lax.dynamic_slice_in_dim(cell_order, round_index * cell_dev, cell_dev)
    support = obs_mask[:, my_cells].astype(jnp.float32)
    partial_sum = jnp.einsum(
        "oc,rcd->od", support, tiles_out.astype(jnp.float32), precision=lax.Precision.HIGHEST
    )
    support_count = round_count * jnp.sum(obs_mask.astype(jnp.float32), axis=1)
    divisor = jnp.sqrt(support_count)
    pooled = lax.psum(partial_sum, ("round", "mp"))
    obs_logits = jnp.dot(pooled, w_read, precision=lax.Precision.HIGHEST) / divisor
    return (tiles_out, obs_logits)


def iota(shape, dimension):
    return lax.broadcasted_iota(jnp.int32, shape, dimension)


def one_hot(condition):
    return jnp.where(condition, 1.0, 0.0).astype(jnp.bfloat16)


def dot(left, right):
    return jnp.dot(left, right, preferred_element_type=jnp.float32)


def dot_t(left, right):
    return lax.dot_general(
        left, right, (((1,), (1,)), ((), ())), preferred_element_type=jnp.float32
    )


def split_three(values):
    high = values.astype(jnp.bfloat16)
    rest = values - high.astype(jnp.float32)
    middle = rest.astype(jnp.bfloat16)
    low = (rest - middle.astype(jnp.float32)).astype(jnp.bfloat16)
    return jnp.concatenate([high, middle, low], axis=0)


def softmax(scores):
    weights = jnp.exp(scores - jnp.max(scores, axis=-1, keepdims=True))
    return (weights / jnp.sum(weights, axis=-1, keepdims=True)).astype(jnp.bfloat16)


def pack_kernel(tokens, seam_rows, block, landed, padded, arrivals):
    cells = tokens.shape[1]
    slots, owners = seam_rows.shape[1:]
    copies = [
        pltpu.make_async_copy(seam_rows.at[0], landed, arrivals.at[0]),
        pltpu.make_async_copy(tokens, block.at[:, :cells], arrivals.at[1]),
    ]
    for copy in copies:
        copy.start()
    padded[...] = jnp.full(padded.shape, -1.0, jnp.float32)
    copies[0].wait()
    padded[:slots, :owners] = landed[...].astype(jnp.float32)
    block[0, cells:, :LANES] = padded[...].astype(jnp.bfloat16)
    copies[1].wait()


def prepare_kernel(rounds, cells, counts, *refs):
    copied, order_in, mask_in = refs[:counts], refs[counts], refs[counts + 1]
    weights, rest = refs[counts + 2 : 2 * counts + 2], refs[2 * counts + 2 :]
    picks, token_picks, of_tile, place_in_tile, tile_bias, divisor = rest[:6]
    order, mask, arrivals = rest[6:]
    copies = [
        pltpu.make_async_copy(source, target, arrivals.at[k])
        for k, (source, target) in enumerate(
            zip((order_in, mask_in, *copied), (order, mask, *weights))
        )
    ]
    for copy in copies:
        copy.start()
    me, model = lax.axis_index("round"), lax.axis_index("mp")
    core, pair = model & 1, lax.shift_right_logical(model, 1)
    cell_dev = cells // rounds
    tile_rows = rounds * cell_dev
    share = tile_rows // 4
    total = rounds * cells
    observables = mask.shape[0]

    def slot_round(slot):
        return me ^ slot ^ jnp.where(slot >= 2, core, 0)

    for copy in copies[:2]:
        copy.wait()
    row = iota((total, 1), 0)
    placed = order[...] == lax.rem(row, cells)
    along = iota((1, cells), 1)
    position = jnp.sum(jnp.where(placed, along, 0), axis=1, keepdims=True)
    tile = lax.div(position, cell_dev)
    in_tile = slot_round(lax.div(row, cells)) * cell_dev + lax.rem(position, cell_dev)
    place_in_tile[...] = jnp.broadcast_to(in_tile.astype(jnp.float32), place_in_tile.shape)
    of_tile[...] = one_hot(tile == slot_round(iota((1, rounds), 1)))
    column = iota((1, total), 1)
    along_rows = jnp.broadcast_to(along.astype(jnp.float32), (8, cells)).astype(jnp.bfloat16)
    position_row = dot_t(along_rows, one_hot(placed))[:1].astype(jnp.int32)
    tile_row = lax.div(position_row, cell_dev)
    in_tile_row = slot_round(lax.div(column, cells)) * cell_dev + lax.rem(position_row, cell_dev)
    tile_bias[...] = jnp.where(tile == tile_row, 0.0, -1e30)

    index = iota((tile_rows, 1), 0)
    quarter = lax.div(index, share)
    target_core = jnp.where(quarter < 2, 1 - core, core)
    target_pair = jnp.where((quarter & 1) == 0, 1 - pair, pair)
    target = (target_pair * 2 + target_core) * share + lax.rem(index, share)
    own = one_hot((tile_row == me) & (in_tile_row == target))
    mask_bf = mask[...].astype(jnp.float32).astype(jnp.bfloat16)
    support = dot(mask_bf, one_hot(iota((cells, 1), 0) == lax.rem(column, cells))).astype(
        jnp.bfloat16
    )
    picks[:tile_rows] = own
    picks[tile_rows:] = support
    token_picks[:tile_rows] = jnp.where(quarter == 3, own, jnp.zeros_like(own))
    token_picks[tile_rows:] = jnp.where(model == 0, support, jnp.zeros_like(support))
    count = rounds * jnp.sum(mask[...].astype(jnp.float32), axis=1, keepdims=True)
    divisor[...] = jnp.broadcast_to(jnp.sqrt(count), divisor.shape)
    for copy in copies[2:]:
        copy.wait()


def layer_kernel(cells, slots, *refs):
    blocks, rest = refs[:slots], refs[slots:]
    gain, w_read, w_query, w_key, w_value, w_gate, w_up, w_down, w_out = rest[:9]
    picks, token_picks, of_tile, place_in_tile, tile_bias, divisor, send, keep = rest[9:]
    total = slots * cells
    width = gain.shape[1]
    head_width = w_query.shape[1]
    observables = divisor.shape[0]
    tile_rows = picks.shape[0] - observables

    tokens = jnp.concatenate([block[0, :cells] for block in blocks], axis=0)
    values = tokens.astype(jnp.float32)
    spread = jnp.mean(values * values, axis=-1, keepdims=True)
    normed = (values * lax.rsqrt(spread + norm_eps) * gain[...]).astype(jnp.bfloat16)

    member = jnp.zeros((total, LANES), jnp.bfloat16)
    for row in (cells, cells + 1):
        table = jnp.concatenate([block[0, row : row + 1, :LANES] for block in blocks], axis=0)
        member = member + one_hot(dot(of_tile[...], table) == place_in_tile[...])
    seam_bias = jnp.where(dot_t(member, member) > 0.5, 0.0, -1e30)
    in_seam = jnp.sum(member.astype(jnp.float32), axis=1, keepdims=True) > 0.5

    queries = dot(normed, w_query[...]).astype(jnp.bfloat16)
    keys = dot(normed, w_key[...]).astype(jnp.bfloat16)
    vals = dot(normed, w_value[...]).astype(jnp.bfloat16)
    gate = dot(normed, w_gate[...])
    up = dot(normed, w_up[...])
    hidden = (gate / (1.0 + jnp.exp(-gate)) * up).astype(jnp.bfloat16)

    scale = 1.0 / math.sqrt(HDIM)
    lane_head = lax.div(iota((1, head_width), 1), HDIM)
    local = jnp.zeros((total, head_width), jnp.float32)
    seam = jnp.zeros((total, head_width), jnp.float32)
    for head in range(head_width // HDIM):
        mine = lane_head == head
        scores = dot_t(queries, jnp.where(mine, keys, jnp.zeros_like(keys))) * scale
        head_vals = jnp.where(mine, vals, jnp.zeros_like(vals))
        local = local + dot(softmax(scores + tile_bias[...]), head_vals)
        seam = seam + dot(softmax(scores + seam_bias), head_vals)
    seam = seam.astype(jnp.bfloat16).astype(jnp.float32)
    combined = (local + jnp.where(in_seam, seam, 0.0)).astype(jnp.bfloat16)

    def last_product(rows, weight):
        own, sums = rows[:tile_rows].astype(jnp.bfloat16), split_three(rows[tile_rows:])
        return dot(jnp.concatenate([own, sums], axis=0), weight)

    product = last_product(dot(picks[...], hidden), w_down[...])
    product = product + last_product(dot(picks[...], combined), w_out[...])
    token_rows = dot(token_picks[...], tokens)
    update = product[:tile_rows] + token_rows[:tile_rows]
    pooled = token_rows[tile_rows:]
    for k in range(3):
        first = tile_rows + observables * k
        pooled = pooled + product[first : first + observables]
    logits = jnp.sum(pooled * w_read[...], axis=1, keepdims=True) / divisor[:, :1]
    diagonal = iota((observables, width), 0) == iota((observables, width), 1)
    logits_row = jnp.sum(jnp.where(diagonal, logits, 0.0), axis=0, keepdims=True)
    half = tile_rows // 2
    for target, rows in ((send, update[:half]), (keep, update[half:])):
        target[:half] = rows
        target[half:] = jnp.broadcast_to(logits_row, (8, width))


def finish_kernel(own, arrived, tiles_out, logits_out):
    count, cell_dev = tiles_out.shape[:2]
    share = count * cell_dev
    rows = own[share : 2 * share] + arrived[:share]
    for k in range(count):
        tiles_out[k] = rows[k * cell_dev : (k + 1) * cell_dev].astype(tiles_out.dtype)
    logits = own[2 * share : 2 * share + 1] + arrived[2 * share : 2 * share + 1]
    logits_out[...] = logits[:, : logits_out.shape[1]]


def shards_whole(
    tokens,
    cell_order,
    seam_rows,
    obs_mask,
    norm_gain,
    w_query,
    w_key,
    w_value,
    w_out,
    w_gate,
    w_up,
    w_down,
    w_read,
):
    rounds = lax.axis_size("round")
    models = lax.axis_size("mp")
    cells, width = tokens.shape[1:]
    cell_dev = cells // rounds
    tile_rows = rounds * cell_dev
    share = tile_rows // models
    total = rounds * cells
    observables = obs_mask.shape[0]
    vmem = pl.BlockSpec(memory_space=pltpu.VMEM)
    hbm = pl.BlockSpec(memory_space=pltpu.HBM)

    def stay(arrays, space):
        return [pltpu.with_memory_space_constraint(array, space) for array in arrays]

    block = pl.pallas_call(
        pack_kernel,
        out_shape=pltpu.VMEM((1, cells + SEAM_PAD, width), jnp.bfloat16),
        in_specs=[hbm, hbm],
        out_specs=vmem,
        scratch_shapes=[
            pltpu.VMEM(seam_rows.shape[:0:-1], jnp.int32),
            pltpu.VMEM((SEAM_PAD, LANES), jnp.float32),
            pltpu.SemaphoreType.DMA((2,)),
        ],
        compiler_params=pltpu.CompilerParams(vmem_limit_bytes=SMALL_LIMIT),
    )(*stay([tokens, seam_rows.transpose(0, 2, 1)], pltpu.HBM))

    def fetch(even_step, odd_step):
        pairs = [
            (r * models + m, (r ^ (odd_step if m & 1 else even_step)) * models + m)
            for r in range(rounds)
            for m in range(models)
        ]
        return lax.ppermute(block, ("round", "mp"), pairs)

    def other_core(array):
        return lax.ppermute(array, "mp", [(m, m ^ 1) for m in range(models)])

    direct = {k: fetch(k, k + 1) for k in range(2, rounds, 2)}
    next_door = fetch(1, 1)
    blocks = [block, next_door]
    for k in range(2, rounds, 2):
        blocks += [direct[k], other_core(direct[k])]

    brought = [
        norm_gain.reshape(1, -1),
        w_read.reshape(1, -1),
        w_query,
        w_key,
        w_value,
        w_gate,
        w_up,
        w_down,
        w_out,
    ]
    prepared = pl.pallas_call(
        functools.partial(prepare_kernel, rounds, cells, len(brought)),
        out_shape=[pltpu.VMEM(array.shape, array.dtype) for array in brought]
        + [
            pltpu.VMEM((tile_rows + observables, total), jnp.bfloat16),
            pltpu.VMEM((tile_rows + observables, total), jnp.bfloat16),
            pltpu.VMEM((total, rounds), jnp.bfloat16),
            pltpu.VMEM((total, LANES), jnp.float32),
            pltpu.VMEM((total, total), jnp.float32),
            pltpu.VMEM((observables, LANES), jnp.float32),
        ],
        in_specs=[hbm] * (len(brought) + 2),
        out_specs=[vmem] * (len(brought) + 6),
        scratch_shapes=[
            pltpu.VMEM((1, cells), jnp.int32),
            pltpu.VMEM(obs_mask.shape, jnp.int32),
            pltpu.SemaphoreType.DMA((len(brought) + 2,)),
        ],
        compiler_params=pltpu.CompilerParams(vmem_limit_bytes=SMALL_LIMIT),
        cost_estimate=pl.CostEstimate(flops=0, bytes_accessed=8 * 1024 * 1024, transcendentals=0),
    )(*stay([*brought, cell_order.reshape(1, -1), obs_mask], pltpu.HBM))

    part = pltpu.VMEM((2 * share + 8, width), jnp.float32)
    send, keep = pl.pallas_call(
        functools.partial(layer_kernel, cells, len(blocks)),
        out_shape=(part, part),
        in_specs=[vmem] * (len(blocks) + len(prepared)),
        out_specs=(vmem, vmem),
        compiler_params=pltpu.CompilerParams(vmem_limit_bytes=LAYER_LIMIT),
    )(*stay([*blocks, *prepared], pltpu.VMEM))
    chip = keep + other_core(send)
    arrived = lax.ppermute(chip, "mp", [(m, m ^ 2) for m in range(models)])
    tiles_out, logits = pl.pallas_call(
        finish_kernel,
        out_shape=(
            jax.ShapeDtypeStruct((share // cell_dev, cell_dev, width), jnp.bfloat16),
            jax.ShapeDtypeStruct((1, observables), jnp.float32),
        ),
        in_specs=[vmem, vmem],
        out_specs=(vmem, vmem),
        compiler_params=pltpu.CompilerParams(vmem_limit_bytes=SMALL_LIMIT),
    )(*stay([chip, arrived], pltpu.VMEM))
    return tiles_out, logits.reshape(-1)


def fits_whole(mesh, tokens, seam_rows, w_query):
    rounds, models = mesh.shape["round"], mesh.shape["mp"]
    total = tokens.shape[0] * tokens.shape[1]
    share = total // rounds // models
    return (
        models == 4
        and rounds == tokens.shape[0]
        and rounds & (rounds - 1) == 0
        and rounds > 2
        and total <= 512
        and total // rounds <= 256
        and share % 8 == 0
        and tokens.shape[1] % 16 == 0
        and seam_rows.shape[2] == 2
        and w_query.shape[1] // models % HDIM == 0
    )


def solution(mesh):
    def layer(*args):
        tokens, seam_rows, w_query = args[0], args[2], args[5]
        whole = fits_whole(mesh, tokens, seam_rows, w_query)
        return placed(mesh, shards_whole if whole else shards_by_tile)(*args)

    return layer


def placed(mesh, shards):
    return jax.shard_map(
        shards,
        mesh=mesh,
        in_specs=(
            P("round", None, None),
            P(),
            P("round", None, None),
            P(),
            P(),
            P(None, "mp"),
            P(None, "mp"),
            P(None, "mp"),
            P("mp", None),
            P(None, "mp"),
            P(None, "mp"),
            P("mp", None),
            P(),
        ),
        out_specs=(P("mp", "round", None), P()),
        check_vma=False,
    )
```

```python
import functools
import math

import jax
import jax.numpy as jnp
from jax import lax
from jax.experimental import pallas as pl
from jax.experimental.pallas import tpu as pltpu
from jax.sharding import PartitionSpec as P

HDIM = 64
LANES = 128
SMALL_LIMIT = 8 * 1024 * 1024
TIED = 0
LAYER_LIMIT = 32 * 1024 * 1024


norm_eps = 1e-06


def normalize(rows_in, norm_gain):
    values = rows_in.astype(jnp.float32)
    spread = jnp.mean(values * values, axis=-1, keepdims=True)
    return (values * lax.rsqrt(spread + norm_eps) * norm_gain).astype(jnp.bfloat16)


def attend(queries, keys_all, values_all, live_keys):
    scale_factor = 1.0 / math.sqrt(queries.shape[-1])
    scores = (
        jnp.einsum("qhe,khe->hqk", queries, keys_all, preferred_element_type=jnp.float32)
        * scale_factor
    )
    if live_keys is not None:
        scores = jnp.where(live_keys[None, None, :], scores, -1e30)
    row_max = jnp.max(scores, axis=-1, keepdims=True)
    weights = jnp.exp(scores - row_max)
    probabilities = (weights / jnp.sum(weights, axis=-1, keepdims=True)).astype(jnp.bfloat16)
    mixture = jnp.einsum(
        "hqk,khe->qhe", probabilities, values_all, preferred_element_type=jnp.float32
    )
    return mixture.reshape(mixture.shape[0], -1)


def shards_by_tile(
    tokens,
    cell_order,
    seam_rows,
    obs_mask,
    norm_gain,
    w_query,
    w_key,
    w_value,
    w_out,
    w_gate,
    w_up,
    w_down,
    w_read,
):
    round_count = lax.axis_size("round")
    model_count = lax.axis_size("mp")
    model_index = lax.axis_index("mp")
    round_index = lax.axis_index("round")
    width = tokens.shape[2]
    cell_dev = tokens.shape[1] // round_count
    permuted = tokens[:, cell_order, :]
    tile_tokens = lax.all_to_all(permuted, "round", split_axis=1, concat_axis=0, tiled=True)
    tile_rows = tile_tokens.shape[0] * cell_dev
    flat_tokens = tile_tokens.reshape(tile_rows, width)
    normed = normalize(flat_tokens, norm_gain)
    queries = jnp.dot(normed, w_query, preferred_element_type=jnp.float32).astype(jnp.bfloat16)
    keys_all = jnp.dot(normed, w_key, preferred_element_type=jnp.float32).astype(jnp.bfloat16)
    values_all = jnp.dot(normed, w_value, preferred_element_type=jnp.float32).astype(jnp.bfloat16)
    head_width = queries.shape[1]
    heads_dev = head_width // HDIM
    block_rows = min(512, tile_rows)
    query_blocks = queries.reshape(tile_rows // block_rows, block_rows, heads_dev, HDIM)
    key_heads = keys_all.reshape(tile_rows, heads_dev, HDIM)
    value_heads = values_all.reshape(tile_rows, heads_dev, HDIM)
    local_attn = lax.map(
        lambda query_block: attend(query_block, key_heads, value_heads, None), query_blocks
    )
    local_attn = local_attn.reshape(tile_rows, head_width)
    live_slot = seam_rows[0] >= 0
    safe_rows = jnp.where(live_slot, seam_rows[0], 0)
    packet = (
        lax.all_to_all(queries[safe_rows], "round", split_axis=0, concat_axis=0, tiled=True),
        lax.all_to_all(keys_all[safe_rows], "round", split_axis=0, concat_axis=0, tiled=True),
        lax.all_to_all(values_all[safe_rows], "round", split_axis=0, concat_axis=0, tiled=True),
        lax.all_to_all(
            live_slot.astype(jnp.bfloat16), "round", split_axis=0, concat_axis=0, tiled=True
        ),
    )
    seam_queries = packet[0].reshape(-1, heads_dev, HDIM)
    seam_keys = packet[1].reshape(-1, heads_dev, HDIM)
    seam_values = packet[2].reshape(-1, heads_dev, HDIM)
    seam_live = packet[3].reshape(-1) > 0.5
    seam_attn = attend(seam_queries, seam_keys, seam_values, seam_live).astype(jnp.bfloat16)
    returned = lax.all_to_all(
        seam_attn.reshape(round_count, -1, head_width),
        "round",
        split_axis=0,
        concat_axis=0,
        tiled=True,
    )
    target = jnp.where(live_slot, seam_rows[0], tile_rows).reshape(-1)
    combined = (
        local_attn.at[target]
        .add(returned.reshape(-1, head_width).astype(jnp.float32), mode="drop")
        .astype(jnp.bfloat16)
    )
    share_rows = tile_rows // model_count
    own_first = model_index * share_rows
    gate_part = jnp.dot(normed, w_gate, preferred_element_type=jnp.float32)
    up_part = jnp.dot(normed, w_up, preferred_element_type=jnp.float32)
    hidden = (jax.nn.silu(gate_part) * up_part).astype(jnp.bfloat16)
    attn_part = jnp.dot(combined, w_out, preferred_element_type=jnp.float32)
    summed = lax.psum_scatter(
        attn_part + jnp.dot(hidden, w_down, preferred_element_type=jnp.float32),
        "mp",
        scatter_dimension=0,
        tiled=True,
    )
    own_rows = lax.dynamic_slice_in_dim(flat_tokens, own_first, share_rows, 0)
    result_rows = (own_rows.astype(jnp.float32) + summed).astype(jnp.bfloat16)
    tiles_out = result_rows.reshape(share_rows // cell_dev, cell_dev, width)
    my_cells = lax.dynamic_slice_in_dim(cell_order, round_index * cell_dev, cell_dev)
    support = obs_mask[:, my_cells].astype(jnp.float32)
    partial_sum = jnp.einsum(
        "oc,rcd->od", support, tiles_out.astype(jnp.float32), precision=lax.Precision.HIGHEST
    )
    support_count = round_count * jnp.sum(obs_mask.astype(jnp.float32), axis=1)
    divisor = jnp.sqrt(support_count)
    pooled = lax.psum(partial_sum, ("round", "mp"))
    obs_logits = jnp.dot(pooled, w_read, precision=lax.Precision.HIGHEST) / divisor
    return (tiles_out, obs_logits)


def iota(shape, dimension):
    return lax.broadcasted_iota(jnp.int32, shape, dimension)


def one_hot(condition):
    return jnp.where(condition, 1.0, 0.0).astype(jnp.bfloat16)


def dot(left, right):
    return jnp.dot(left, right, preferred_element_type=jnp.float32)


def dot_t(left, right):
    return lax.dot_general(
        left, right, (((1,), (1,)), ((), ())), preferred_element_type=jnp.float32
    )


def split_three(values):
    high = values.astype(jnp.bfloat16)
    rest = values - high.astype(jnp.float32)
    middle = rest.astype(jnp.bfloat16)
    low = (rest - middle.astype(jnp.float32)).astype(jnp.bfloat16)
    return jnp.concatenate([high, middle, low], axis=0)


def softmax(scores):
    weights = jnp.exp(scores - jnp.max(scores, axis=0, keepdims=True))
    return (weights / jnp.sum(weights, axis=0, keepdims=True)).astype(jnp.bfloat16)


def fetch_steps(rounds):
    shifts = [2, *range(rounds - 2, 2, -2)]
    return [((k, 0), (k, 1)) for k in shifts] + [((0, 1), (0, 1))]


def slot_steps(rounds):
    steps = [((0, 0), (0, 0))]
    for even, odd in fetch_steps(rounds):
        steps += [(even, odd)] if even == odd else [(even, odd), (odd, even)]
    return steps


def pack_kernel(prepare, given, made, tokens, seam_rows, *refs):
    block, (landed, padded, arrivals) = refs[given], refs[-3:]
    width = tokens.shape[2]
    slots, owners = seam_rows.shape[1:]
    copies = [
        pltpu.make_async_copy(seam_rows.at[0], landed, arrivals.at[0]),
        pltpu.make_async_copy(tokens, block.at[:, :, :width], arrivals.at[1]),
    ]
    for copy in copies:
        copy.start()
    padded[...] = jnp.zeros(padded.shape, jnp.float32)
    copies[0].wait()
    row = iota((tokens.shape[1], owners), 0)
    held = row == landed[:1]
    for slot in range(1, slots):
        held = held | (row == landed[slot : slot + 1])
    padded[:, :owners] = jnp.where(held, 1.0, 0.0)
    block[0, :, width:] = padded[...].astype(jnp.bfloat16)
    copies[1].wait()

    @pl.when(lax.axis_index("round") == 0)
    def _():
        prepare(*refs[:given], *refs[given + 1 : given + 1 + made], *refs[given + 1 + made : -3])


def late_kernel(prepare, given, made, *refs):
    @pl.when(lax.axis_index("round") != 0)
    def _():
        prepare(*refs[:given], *refs[given + made :])


def prepare(rounds, cells, counts, *refs):
    order_in, mask_in, *copied = refs[: counts + 2]
    rest = refs[counts + 2 :]
    gain, w_read, w_query, w_key, w_gate, w_up, w_down, w_out = rest[:8]
    w_value_t, read_down, read_out = rest[8:11]
    picks, token_picks, place, tile_bias, divisor = rest[11:16]
    order, mask, w_value, arrivals = rest[16:]
    targets = (order, mask, gain, w_read, w_value, w_query, w_key, w_gate, w_up, w_down, w_out)
    copies = [
        pltpu.make_async_copy(source, target, arrivals.at[k])
        for k, (source, target) in enumerate(zip((order_in, mask_in, *copied), targets))
    ]
    for copy in copies:
        copy.start()
    me, model = lax.axis_index("round"), lax.axis_index("mp")
    core, pair = model & 1, lax.shift_right_logical(model, 1)
    cell_dev = cells // rounds
    tile_rows = rounds * cell_dev
    share = tile_rows // 4
    total = rounds * cells
    observables = mask.shape[0]

    def slot_round(slot):
        shift, flip = jnp.zeros_like(slot), jnp.zeros_like(slot)
        for k, (even, odd) in enumerate(slot_steps(rounds)):
            shift = jnp.where(slot == k, jnp.where(core == 0, even[0], odd[0]), shift)
            flip = jnp.where(slot == k, jnp.where(core == 0, even[1], odd[1]), flip)
        return ((me + rounds - shift) & (rounds - 1)) ^ flip

    for copy in copies[:2]:
        copy.wait()
    row = iota((total, 1), 0)
    placed = order[...] == lax.rem(row, cells)
    along = iota((1, cells), 1)
    position = jnp.sum(jnp.where(placed, along, 0), axis=1, keepdims=True)
    tile = lax.div(position, cell_dev)
    in_tile = slot_round(lax.div(row, cells)) * cell_dev + lax.rem(position, cell_dev)
    column = iota((1, total), 1)
    slot_start = slot_round(lax.div(column, cells)) * tile_rows
    place[...] = one_hot(tile * tile_rows + in_tile == slot_start + lax.rem(column, cells))
    along_rows = jnp.broadcast_to(along.astype(jnp.float32), (8, cells)).astype(jnp.bfloat16)
    position_row = dot_t(along_rows, one_hot(placed))[:1].astype(jnp.int32)
    tile_row = lax.div(position_row, cell_dev)
    in_tile_row = slot_round(lax.div(column, cells)) * cell_dev + lax.rem(position_row, cell_dev)
    tile_bias[...] = jnp.where(tile == tile_row, 0.0, -1e30)

    index = iota((tile_rows, 1), 0)
    quarter = lax.div(index, share)
    target_core = jnp.where(quarter < 2, 1 - core, core)
    target_pair = jnp.where((quarter & 1) == 0, 1 - pair, pair)
    target = (target_pair * 2 + target_core) * share + lax.rem(index, share)
    own = one_hot((tile_row == me) & (in_tile_row == target))
    mask_bf = mask[...].astype(jnp.float32).astype(jnp.bfloat16)
    support = dot(mask_bf, one_hot(iota((cells, 1), 0) == lax.rem(column, cells))).astype(
        jnp.bfloat16
    )
    picks[:tile_rows] = own
    picks[tile_rows:] = support
    token_picks[:tile_rows] = jnp.where(quarter == 3, own, jnp.zeros_like(own))
    token_picks[tile_rows:] = jnp.where(model == 0, support, jnp.zeros_like(support))
    count = rounds * jnp.sum(mask[...].astype(jnp.float32), axis=1, keepdims=True)
    divisor[...] = jnp.broadcast_to(jnp.sqrt(count), divisor.shape)

    for copy in copies[2:5]:
        copy.wait()
    head_width = w_value.shape[1]
    identity = one_hot(iota((head_width, 1), 0) == iota((1, head_width), 1))
    w_value_t[...] = dot_t(identity, w_value[...]).astype(jnp.bfloat16)
    read_parts = split_three(jnp.broadcast_to(w_read[...], (8, w_read.shape[1])))
    for copy in copies[5:]:
        copy.wait()
    for weight, read in ((w_down, read_down), (w_out, read_out)):
        parts = dot_t(read_parts, weight[...])
        read[...] = parts[:1] + parts[8:9] + parts[16:17]


def layer_kernel(cells, slots, *refs):
    blocks, rest = refs[:slots], refs[slots:]
    gain, w_read, w_query, w_key, w_gate, w_up, w_down, w_out = rest[:8]
    w_value_t, read_down, read_out = rest[8:11]
    picks, token_picks, place, tile_bias, divisor = rest[11:16]
    outs = rest[16:]
    total = slots * cells
    width = gain.shape[1]
    head_width = w_query.shape[1]
    observables = divisor.shape[0]
    tile_rows = picks.shape[0] - observables

    tokens = jnp.concatenate([block[0, :, :width] for block in blocks], axis=0)
    values = tokens.astype(jnp.float32)
    spread = jnp.mean(values * values, axis=-1, keepdims=True)
    normed = (values * lax.rsqrt(spread + norm_eps) * gain[...]).astype(jnp.bfloat16)

    members = jnp.concatenate([block[0, :, width:] for block in blocks], axis=0)
    member = dot(place[...], members).astype(jnp.bfloat16)
    seam_bias = jnp.where(dot_t(member, member) > 0.5, 0.0, -1e30)
    in_seam = dot_t(jnp.ones((8, LANES), jnp.bfloat16), member)[:1] > 0.5

    gate = dot(normed, w_gate[...])
    up = dot(normed, w_up[...])
    hidden = (gate / (1.0 + jnp.exp(-gate)) * up).astype(jnp.bfloat16)

    queries = (dot(normed, w_query[...]) * (1.0 / math.sqrt(HDIM))).astype(jnp.bfloat16)
    keys = dot(normed, w_key[...]).astype(jnp.bfloat16)
    vals = dot_t(w_value_t[...], normed).astype(jnp.bfloat16)
    lane_head = lax.div(iota((1, head_width), 1), HDIM)
    heads = []
    for head in range(head_width // HDIM):
        head_keys = jnp.where(lane_head == head, keys, jnp.zeros_like(keys))
        head_vals = vals[head * HDIM : (head + 1) * HDIM]
        parts = []
        for first in range(0, total, LANES):
            some = slice(first, first + LANES)
            scores = dot_t(head_keys, queries[some])
            local = dot(head_vals, softmax(scores + tile_bias[:, some]))
            seam = dot(head_vals, softmax(scores + seam_bias[:, some]))
            seam = seam.astype(jnp.bfloat16).astype(jnp.float32)
            parts.append((local + jnp.where(in_seam[:, some], seam, 0.0)).astype(jnp.bfloat16))
        heads.append(jnp.concatenate(parts, axis=1))
    combined = jnp.concatenate(heads, axis=0)

    hidden_rows = dot(picks[...], hidden)
    combined_rows = dot_t(picks[...], combined)
    token_rows = dot(token_picks[...], tokens)
    update = (
        token_rows[:tile_rows]
        + dot(hidden_rows[:tile_rows].astype(jnp.bfloat16), w_down[...])
        + dot(combined_rows[:tile_rows].astype(jnp.bfloat16), w_out[...])
    )
    logits = sum(
        jnp.sum(sums[tile_rows:] * read[...], axis=1, keepdims=True)
        for sums, read in (
            (hidden_rows, read_down),
            (combined_rows, read_out),
            (token_rows, w_read),
        )
    )
    logits = logits / divisor[:, :1]
    diagonal = iota((observables, LANES), 0) == iota((observables, LANES), 1)
    logits_row = jnp.sum(jnp.where(diagonal, logits, 0.0), axis=0, keepdims=True)
    share = tile_rows // 4
    send_over, send_stay, keep_over, keep_stay = outs
    for k, (over, stay) in enumerate(((send_over, send_stay), (keep_over, keep_stay))):
        over[:, :width] = update[2 * k * share : (2 * k + 1) * share]
        over[:, width:] = jnp.broadcast_to(logits_row, (share, LANES))
        stay[...] = update[(2 * k + 1) * share : (2 * k + 2) * share]


def finish_kernel(over, arrived, stay, other_stay, tiles_out, logits_out):
    count, cell_dev = tiles_out.shape[:2]
    width = stay.shape[1]
    rows = stay[...] + other_stay[...] + arrived[:, :width]
    for k in range(count):
        tiles_out[k] = rows[k * cell_dev : (k + 1) * cell_dev].astype(tiles_out.dtype)
    logits = over[:1, width:] + arrived[:1, width:]
    logits_out[...] = logits[:, : logits_out.shape[1]]


def shards_whole(
    tokens,
    cell_order,
    seam_rows,
    obs_mask,
    norm_gain,
    w_query,
    w_key,
    w_value,
    w_out,
    w_gate,
    w_up,
    w_down,
    w_read,
):
    rounds = lax.axis_size("round")
    models = lax.axis_size("mp")
    cells, width = tokens.shape[1:]
    cell_dev = cells // rounds
    tile_rows = rounds * cell_dev
    share = tile_rows // models
    total = rounds * cells
    observables = obs_mask.shape[0]
    vmem = pl.BlockSpec(memory_space=pltpu.VMEM)
    hbm = pl.BlockSpec(memory_space=pltpu.HBM)

    def pin(arrays, space):
        return [pltpu.with_memory_space_constraint(array, space) for array in arrays]

    brought = [
        norm_gain.reshape(1, -1),
        w_read.reshape(1, -1),
        w_value,
        w_query,
        w_key,
        w_gate,
        w_up,
        w_down,
        w_out,
    ]
    sources = pin([cell_order.reshape(1, -1), obs_mask, *brought], pltpu.HBM)
    made = [pltpu.VMEM(array.shape, array.dtype) for k, array in enumerate(brought) if k != 2] + [
        pltpu.VMEM(w_value.shape[::-1], w_value.dtype),
        pltpu.VMEM((1, w_down.shape[0]), jnp.float32),
        pltpu.VMEM((1, w_out.shape[0]), jnp.float32),
        pltpu.VMEM((tile_rows + observables, total), jnp.bfloat16),
        pltpu.VMEM((tile_rows + observables, total), jnp.bfloat16),
        pltpu.VMEM((total, total), jnp.bfloat16),
        pltpu.VMEM((total, total), jnp.float32),
        pltpu.VMEM((observables, LANES), jnp.float32),
    ]
    scratch = [
        pltpu.VMEM((1, cells), jnp.int32),
        pltpu.VMEM(obs_mask.shape, jnp.int32),
        pltpu.VMEM(w_value.shape, w_value.dtype),
        pltpu.SemaphoreType.DMA((len(sources),)),
    ]
    small = pltpu.CompilerParams(vmem_limit_bytes=SMALL_LIMIT)
    preparation = functools.partial(prepare, rounds, cells, len(brought))
    block, *prepared = pl.pallas_call(
        functools.partial(pack_kernel, preparation, len(sources), len(made)),
        out_shape=[pltpu.VMEM((1, cells, width + LANES), jnp.bfloat16), *made],
        in_specs=[hbm] * (len(sources) + 2),
        out_specs=[vmem] * (len(made) + 1),
        scratch_shapes=[
            *scratch,
            pltpu.VMEM(seam_rows.shape[:0:-1], jnp.int32),
            pltpu.VMEM((cells, LANES), jnp.float32),
            pltpu.SemaphoreType.DMA((2,)),
        ],
        compiler_params=small,
    )(*pin([tokens, seam_rows.transpose(0, 2, 1)], pltpu.HBM), *sources)

    def fetch(even, odd):
        pairs = []
        for r in range(rounds):
            for m in range(models):
                shift, flip = odd if m & 1 else even
                pairs.append(((((r - shift) % rounds) ^ flip) * models + m, r * models + m))
        return lax.ppermute(block, ("round", "mp"), pairs)

    def other_core(array):
        return lax.ppermute(array, "mp", [(m, m ^ 1) for m in range(models)])

    direct = [fetch(even, odd) for even, odd in fetch_steps(rounds)]
    prepared = pl.pallas_call(
        functools.partial(late_kernel, preparation, len(sources), len(made)),
        out_shape=made,
        in_specs=[hbm] * len(sources) + [vmem] * len(made),
        out_specs=[vmem] * len(made),
        input_output_aliases={len(sources) + k: k for k in range(len(made))},
        scratch_shapes=scratch,
        compiler_params=small,
        cost_estimate=pl.CostEstimate(flops=0, bytes_accessed=8 * 1024 * 1024, transcendentals=0),
    )(*sources, *pin(prepared, pltpu.VMEM))

    direct[TIED], prepared = lax.optimization_barrier((direct[TIED], prepared))
    blocks = [block]
    for (even, odd), fetched in zip(fetch_steps(rounds), direct):
        blocks += [fetched] if even == odd else [fetched, other_core(fetched)]

    over = pltpu.VMEM((share, width + LANES), jnp.float32)
    stay = pltpu.VMEM((share, width), jnp.float32)
    send_over, send_stay, keep_over, keep_stay = pl.pallas_call(
        functools.partial(layer_kernel, cells, len(blocks)),
        out_shape=(over, stay, over, stay),
        in_specs=[vmem] * (len(blocks) + len(prepared)),
        out_specs=(vmem,) * 4,
        compiler_params=pltpu.CompilerParams(vmem_limit_bytes=LAYER_LIMIT),
    )(*pin([*blocks, *prepared], pltpu.VMEM))
    over = keep_over + other_core(send_over)
    arrived = lax.ppermute(over, "mp", [(m, m ^ 2) for m in range(models)])
    other_stay = other_core(send_stay)
    tiles_out, logits = pl.pallas_call(
        finish_kernel,
        out_shape=(
            jax.ShapeDtypeStruct((share // cell_dev, cell_dev, width), jnp.bfloat16),
            jax.ShapeDtypeStruct((1, observables), jnp.float32),
        ),
        in_specs=[vmem] * 4,
        out_specs=(vmem, vmem),
        compiler_params=pltpu.CompilerParams(vmem_limit_bytes=SMALL_LIMIT),
    )(*pin([over, arrived, keep_stay, other_stay], pltpu.VMEM))
    return tiles_out, logits.reshape(-1)


def fits_whole(mesh, tokens, seam_rows, w_query):
    rounds, models = mesh.shape["round"], mesh.shape["mp"]
    total = tokens.shape[0] * tokens.shape[1]
    share = total // rounds // models
    return (
        models == 4
        and rounds == tokens.shape[0]
        and rounds & (rounds - 1) == 0
        and rounds > 2
        and total <= 512
        and total % LANES == 0
        and total // rounds <= 256
        and share % 8 == 0
        and tokens.shape[1] % 16 == 0
        and seam_rows.shape[2] == 2
        and w_query.shape[1] // models % HDIM == 0
    )


def solution(mesh):
    def layer(*args):
        tokens, seam_rows, w_query = args[0], args[2], args[5]
        whole = fits_whole(mesh, tokens, seam_rows, w_query)
        return placed(mesh, shards_whole if whole else shards_by_tile)(*args)

    return layer


def placed(mesh, shards):
    return jax.shard_map(
        shards,
        mesh=mesh,
        in_specs=(
            P("round", None, None),
            P(),
            P("round", None, None),
            P(),
            P(),
            P(None, "mp"),
            P(None, "mp"),
            P(None, "mp"),
            P("mp", None),
            P(None, "mp"),
            P(None, "mp"),
            P("mp", None),
            P(),
        ),
        out_specs=(P("mp", "round", None), P()),
        check_vma=False,
    )
```

```python
import functools
import math

import jax
import jax.numpy as jnp
from jax import lax
from jax.experimental import pallas as pl
from jax.experimental.pallas import tpu as pltpu
from jax.sharding import PartitionSpec as P

HDIM = 64
LANES = 128
SMALL_LIMIT = 8 * 1024 * 1024
TIED = 0
LAYER_LIMIT = 32 * 1024 * 1024


norm_eps = 1e-06


def normalize(rows_in, norm_gain):
    values = rows_in.astype(jnp.float32)
    spread = jnp.mean(values * values, axis=-1, keepdims=True)
    return (values * lax.rsqrt(spread + norm_eps) * norm_gain).astype(jnp.bfloat16)


def attend(queries, keys_all, values_all, live_keys):
    scale_factor = 1.0 / math.sqrt(queries.shape[-1])
    scores = (
        jnp.einsum("qhe,khe->hqk", queries, keys_all, preferred_element_type=jnp.float32)
        * scale_factor
    )
    if live_keys is not None:
        scores = jnp.where(live_keys[None, None, :], scores, -1e30)
    row_max = jnp.max(scores, axis=-1, keepdims=True)
    weights = jnp.exp(scores - row_max)
    probabilities = (weights / jnp.sum(weights, axis=-1, keepdims=True)).astype(jnp.bfloat16)
    mixture = jnp.einsum(
        "hqk,khe->qhe", probabilities, values_all, preferred_element_type=jnp.float32
    )
    return mixture.reshape(mixture.shape[0], -1)


def shards_by_tile(
    tokens,
    cell_order,
    seam_rows,
    obs_mask,
    norm_gain,
    w_query,
    w_key,
    w_value,
    w_out,
    w_gate,
    w_up,
    w_down,
    w_read,
):
    round_count = lax.axis_size("round")
    model_count = lax.axis_size("mp")
    model_index = lax.axis_index("mp")
    round_index = lax.axis_index("round")
    width = tokens.shape[2]
    cell_dev = tokens.shape[1] // round_count
    permuted = tokens[:, cell_order, :]
    tile_tokens = lax.all_to_all(permuted, "round", split_axis=1, concat_axis=0, tiled=True)
    tile_rows = tile_tokens.shape[0] * cell_dev
    flat_tokens = tile_tokens.reshape(tile_rows, width)
    normed = normalize(flat_tokens, norm_gain)
    queries = jnp.dot(normed, w_query, preferred_element_type=jnp.float32).astype(jnp.bfloat16)
    keys_all = jnp.dot(normed, w_key, preferred_element_type=jnp.float32).astype(jnp.bfloat16)
    values_all = jnp.dot(normed, w_value, preferred_element_type=jnp.float32).astype(jnp.bfloat16)
    head_width = queries.shape[1]
    heads_dev = head_width // HDIM
    block_rows = min(512, tile_rows)
    query_blocks = queries.reshape(tile_rows // block_rows, block_rows, heads_dev, HDIM)
    key_heads = keys_all.reshape(tile_rows, heads_dev, HDIM)
    value_heads = values_all.reshape(tile_rows, heads_dev, HDIM)
    local_attn = lax.map(
        lambda query_block: attend(query_block, key_heads, value_heads, None), query_blocks
    )
    local_attn = local_attn.reshape(tile_rows, head_width)
    live_slot = seam_rows[0] >= 0
    safe_rows = jnp.where(live_slot, seam_rows[0], 0)
    packet = (
        lax.all_to_all(queries[safe_rows], "round", split_axis=0, concat_axis=0, tiled=True),
        lax.all_to_all(keys_all[safe_rows], "round", split_axis=0, concat_axis=0, tiled=True),
        lax.all_to_all(values_all[safe_rows], "round", split_axis=0, concat_axis=0, tiled=True),
        lax.all_to_all(
            live_slot.astype(jnp.bfloat16), "round", split_axis=0, concat_axis=0, tiled=True
        ),
    )
    seam_queries = packet[0].reshape(-1, heads_dev, HDIM)
    seam_keys = packet[1].reshape(-1, heads_dev, HDIM)
    seam_values = packet[2].reshape(-1, heads_dev, HDIM)
    seam_live = packet[3].reshape(-1) > 0.5
    seam_attn = attend(seam_queries, seam_keys, seam_values, seam_live).astype(jnp.bfloat16)
    returned = lax.all_to_all(
        seam_attn.reshape(round_count, -1, head_width),
        "round",
        split_axis=0,
        concat_axis=0,
        tiled=True,
    )
    target = jnp.where(live_slot, seam_rows[0], tile_rows).reshape(-1)
    combined = (
        local_attn.at[target]
        .add(returned.reshape(-1, head_width).astype(jnp.float32), mode="drop")
        .astype(jnp.bfloat16)
    )
    share_rows = tile_rows // model_count
    own_first = model_index * share_rows
    gate_part = jnp.dot(normed, w_gate, preferred_element_type=jnp.float32)
    up_part = jnp.dot(normed, w_up, preferred_element_type=jnp.float32)
    hidden = (jax.nn.silu(gate_part) * up_part).astype(jnp.bfloat16)
    attn_part = jnp.dot(combined, w_out, preferred_element_type=jnp.float32)
    summed = lax.psum_scatter(
        attn_part + jnp.dot(hidden, w_down, preferred_element_type=jnp.float32),
        "mp",
        scatter_dimension=0,
        tiled=True,
    )
    own_rows = lax.dynamic_slice_in_dim(flat_tokens, own_first, share_rows, 0)
    result_rows = (own_rows.astype(jnp.float32) + summed).astype(jnp.bfloat16)
    tiles_out = result_rows.reshape(share_rows // cell_dev, cell_dev, width)
    my_cells = lax.dynamic_slice_in_dim(cell_order, round_index * cell_dev, cell_dev)
    support = obs_mask[:, my_cells].astype(jnp.float32)
    partial_sum = jnp.einsum(
        "oc,rcd->od", support, tiles_out.astype(jnp.float32), precision=lax.Precision.HIGHEST
    )
    support_count = round_count * jnp.sum(obs_mask.astype(jnp.float32), axis=1)
    divisor = jnp.sqrt(support_count)
    pooled = lax.psum(partial_sum, ("round", "mp"))
    obs_logits = jnp.dot(pooled, w_read, precision=lax.Precision.HIGHEST) / divisor
    return (tiles_out, obs_logits)


def iota(shape, dimension):
    return lax.broadcasted_iota(jnp.int32, shape, dimension)


def one_hot(condition):
    return jnp.where(condition, 1.0, 0.0).astype(jnp.bfloat16)


def dot(left, right):
    return jnp.dot(left, right, preferred_element_type=jnp.float32)


def dot_t(left, right):
    return lax.dot_general(
        left, right, (((1,), (1,)), ((), ())), preferred_element_type=jnp.float32
    )


def split_three(values):
    high = values.astype(jnp.bfloat16)
    rest = values - high.astype(jnp.float32)
    middle = rest.astype(jnp.bfloat16)
    low = (rest - middle.astype(jnp.float32)).astype(jnp.bfloat16)
    return jnp.concatenate([high, middle, low], axis=0)


def attend_by_keys(head_vals, scores):
    weights = jnp.exp(scores - jnp.max(scores, axis=0, keepdims=True))
    probabilities = (weights / jnp.sum(weights, axis=0, keepdims=True)).astype(jnp.bfloat16)
    return dot(head_vals, probabilities)


def fetch_steps(rounds):
    shifts = [2, *range(rounds - 2, 2, -2)]
    return [((k, 0), (k, 1)) for k in shifts] + [((0, 1), (0, 1))]


def slot_steps(rounds):
    steps = [((0, 0), (0, 0))]
    for even, odd in fetch_steps(rounds):
        steps += [(even, odd)] if even == odd else [(even, odd), (odd, even)]
    return steps


def pack_kernel(prepare, given, made, tokens, seam_rows, *refs):
    block, (landed, padded, arrivals) = refs[given], refs[-3:]
    width = tokens.shape[2]
    slots, owners = seam_rows.shape[1:]
    copies = [
        pltpu.make_async_copy(seam_rows.at[0], landed, arrivals.at[0]),
        pltpu.make_async_copy(tokens, block.at[:, :, :width], arrivals.at[1]),
    ]
    for copy in copies:
        copy.start()
    padded[...] = jnp.zeros(padded.shape, jnp.float32)
    copies[0].wait()
    row = iota((tokens.shape[1], owners), 0)
    held = row == landed[:1]
    for slot in range(1, slots):
        held = held | (row == landed[slot : slot + 1])
    padded[:, :owners] = jnp.where(held, 1.0, 0.0)
    block[0, :, width:] = padded[...].astype(jnp.bfloat16)
    copies[1].wait()

    @pl.when(lax.axis_index("round") == 0)
    def _():
        prepare(*refs[:given], *refs[given + 1 : given + 1 + made], *refs[given + 1 + made : -3])


def late_kernel(prepare, given, made, *refs):
    @pl.when(lax.axis_index("round") != 0)
    def _():
        prepare(*refs[:given], *refs[given + made :])


def prepare(rounds, cells, counts, *refs):
    order_in, mask_in, *copied = refs[: counts + 2]
    rest = refs[counts + 2 :]
    gain, w_read, w_query, w_key, w_gate, w_up, w_down, w_out = rest[:8]
    w_value_t, read_down, read_out = rest[8:11]
    picks, token_picks, place, tile_bias, divisor = rest[11:16]
    order, mask, w_value, arrivals = rest[16:]
    targets = (order, mask, gain, w_read, w_value, w_query, w_key, w_gate, w_up, w_down, w_out)
    copies = [
        pltpu.make_async_copy(source, target, arrivals.at[k])
        for k, (source, target) in enumerate(zip((order_in, mask_in, *copied), targets))
    ]
    for copy in copies:
        copy.start()
    me, model = lax.axis_index("round"), lax.axis_index("mp")
    core, pair = model & 1, lax.shift_right_logical(model, 1)
    cell_dev = cells // rounds
    tile_rows = rounds * cell_dev
    share = tile_rows // 4
    total = rounds * cells
    observables = mask.shape[0]

    def slot_round(slot):
        shift, flip = jnp.zeros_like(slot), jnp.zeros_like(slot)
        for k, (even, odd) in enumerate(slot_steps(rounds)):
            shift = jnp.where(slot == k, jnp.where(core == 0, even[0], odd[0]), shift)
            flip = jnp.where(slot == k, jnp.where(core == 0, even[1], odd[1]), flip)
        return ((me + rounds - shift) & (rounds - 1)) ^ flip

    for copy in copies[:2]:
        copy.wait()
    row = iota((total, 1), 0)
    placed = order[...] == lax.rem(row, cells)
    along = iota((1, cells), 1)
    position = jnp.sum(jnp.where(placed, along, 0), axis=1, keepdims=True)
    tile = lax.div(position, cell_dev)
    in_tile = slot_round(lax.div(row, cells)) * cell_dev + lax.rem(position, cell_dev)
    column = iota((1, total), 1)
    slot_start = slot_round(lax.div(column, cells)) * tile_rows
    place[...] = one_hot(tile * tile_rows + in_tile == slot_start + lax.rem(column, cells))
    along_rows = jnp.broadcast_to(along.astype(jnp.float32), (8, cells)).astype(jnp.bfloat16)
    position_row = dot_t(along_rows, one_hot(placed))[:1].astype(jnp.int32)
    tile_row = lax.div(position_row, cell_dev)
    in_tile_row = slot_round(lax.div(column, cells)) * cell_dev + lax.rem(position_row, cell_dev)
    tile_bias[...] = jnp.where(tile == tile_row, 0.0, -1e30)

    index = iota((tile_rows, 1), 0)
    quarter = lax.div(index, share)
    target_core = jnp.where(quarter < 2, 1 - core, core)
    target_pair = jnp.where((quarter & 1) == 0, 1 - pair, pair)
    target = (target_pair * 2 + target_core) * share + lax.rem(index, share)
    own = one_hot((tile_row == me) & (in_tile_row == target))
    mask_bf = mask[...].astype(jnp.float32).astype(jnp.bfloat16)
    support = dot(mask_bf, one_hot(iota((cells, 1), 0) == lax.rem(column, cells))).astype(
        jnp.bfloat16
    )
    picks[:tile_rows] = own
    picks[tile_rows:] = support
    token_picks[:tile_rows] = jnp.where(quarter == 3, own, jnp.zeros_like(own))
    token_picks[tile_rows:] = jnp.where(model == 0, support, jnp.zeros_like(support))
    count = rounds * jnp.sum(mask[...].astype(jnp.float32), axis=1, keepdims=True)
    divisor[...] = jnp.broadcast_to(jnp.sqrt(count), divisor.shape)

    for copy in copies[2:5]:
        copy.wait()
    head_width = w_value.shape[1]
    identity = one_hot(iota((head_width, 1), 0) == iota((1, head_width), 1))
    w_value_t[...] = dot_t(identity, w_value[...]).astype(jnp.bfloat16)
    read_parts = split_three(jnp.broadcast_to(w_read[...], (8, w_read.shape[1])))
    for copy in copies[5:]:
        copy.wait()
    for weight, read in ((w_down, read_down), (w_out, read_out)):
        parts = dot_t(read_parts, weight[...])
        read[...] = parts[:1] + parts[8:9] + parts[16:17]


def layer_kernel(cells, slots, *refs):
    blocks, rest = refs[:slots], refs[slots:]
    gain, w_read, w_query, w_key, w_gate, w_up, w_down, w_out = rest[:8]
    w_value_t, read_down, read_out = rest[8:11]
    picks, token_picks, place, tile_bias, divisor = rest[11:16]
    outs = rest[16:]
    total = slots * cells
    width = gain.shape[1]
    head_width = w_query.shape[1]
    observables = divisor.shape[0]
    tile_rows = picks.shape[0] - observables

    tokens = jnp.concatenate([block[0, :, :width] for block in blocks], axis=0)
    token_rows = dot(token_picks[...], tokens)

    members = jnp.concatenate([block[0, :, width:] for block in blocks], axis=0)
    member = dot(place[...], members).astype(jnp.bfloat16)

    values = tokens.astype(jnp.float32)
    spread = jnp.mean(values * values, axis=-1, keepdims=True)
    normed = (values * lax.rsqrt(spread + norm_eps) * gain[...]).astype(jnp.bfloat16)

    queries = (dot(normed, w_query[...]) * (1.0 / math.sqrt(HDIM))).astype(jnp.bfloat16)
    keys = dot(normed, w_key[...]).astype(jnp.bfloat16)
    vals = dot_t(w_value_t[...], normed).astype(jnp.bfloat16)

    gate = dot(normed, w_gate[...])
    up = dot(normed, w_up[...])
    hidden = (gate / (1.0 + jnp.exp(-gate)) * up).astype(jnp.bfloat16)

    seam_bias = jnp.where(dot_t(member, member) > 0.5, 0.0, -1e30)
    in_seam = dot_t(jnp.ones((8, LANES), jnp.bfloat16), member)[:1] > 0.5
    lane_head = lax.div(iota((1, head_width), 1), HDIM)
    parts = []
    for first in range(0, total, LANES):
        some = slice(first, first + LANES)
        mixed = []
        for head in range(head_width // HDIM):
            head_keys = jnp.where(lane_head == head, keys, jnp.zeros_like(keys))
            head_vals = vals[head * HDIM : (head + 1) * HDIM]
            scores = dot_t(head_keys, queries[some])
            local = attend_by_keys(head_vals, scores + tile_bias[:, some])
            seam = attend_by_keys(head_vals, scores + seam_bias[:, some])
            seam = seam.astype(jnp.bfloat16).astype(jnp.float32)
            mixed.append((local + jnp.where(in_seam[:, some], seam, 0.0)).astype(jnp.bfloat16))
        parts.append(jnp.concatenate(mixed, axis=0))
    combined = jnp.concatenate(parts, axis=1)

    hidden_rows = dot(picks[...], hidden)
    combined_rows = dot_t(picks[...], combined)
    update = (
        token_rows[:tile_rows]
        + dot(hidden_rows[:tile_rows].astype(jnp.bfloat16), w_down[...])
        + dot(combined_rows[:tile_rows].astype(jnp.bfloat16), w_out[...])
    )
    logits = sum(
        jnp.sum(sums[tile_rows:] * read[...], axis=1, keepdims=True)
        for sums, read in (
            (hidden_rows, read_down),
            (combined_rows, read_out),
            (token_rows, w_read),
        )
    )
    logits = logits / divisor[:, :1]
    diagonal = iota((observables, LANES), 0) == iota((observables, LANES), 1)
    logits_row = jnp.sum(jnp.where(diagonal, logits, 0.0), axis=0, keepdims=True)
    share = tile_rows // 4
    send_over, send_stay, keep_over, keep_stay = outs
    for k, (over, stay) in enumerate(((send_over, send_stay), (keep_over, keep_stay))):
        over[:, :width] = update[2 * k * share : (2 * k + 1) * share]
        over[:, width:] = jnp.broadcast_to(logits_row, (share, LANES))
        stay[...] = update[(2 * k + 1) * share : (2 * k + 2) * share]


def finish_kernel(over, arrived, stay, other_stay, tiles_out, logits_out):
    count, cell_dev = tiles_out.shape[:2]
    width = stay.shape[1]
    rows = stay[...] + other_stay[...] + arrived[:, :width]
    for k in range(count):
        tiles_out[k] = rows[k * cell_dev : (k + 1) * cell_dev].astype(tiles_out.dtype)
    logits = over[:1, width:] + arrived[:1, width:]
    logits_out[...] = logits[:, : logits_out.shape[1]]


def shards_whole(
    tokens,
    cell_order,
    seam_rows,
    obs_mask,
    norm_gain,
    w_query,
    w_key,
    w_value,
    w_out,
    w_gate,
    w_up,
    w_down,
    w_read,
):
    rounds = lax.axis_size("round")
    models = lax.axis_size("mp")
    cells, width = tokens.shape[1:]
    cell_dev = cells // rounds
    tile_rows = rounds * cell_dev
    share = tile_rows // models
    total = rounds * cells
    observables = obs_mask.shape[0]
    vmem = pl.BlockSpec(memory_space=pltpu.VMEM)
    hbm = pl.BlockSpec(memory_space=pltpu.HBM)

    def pin(arrays, space):
        return [pltpu.with_memory_space_constraint(array, space) for array in arrays]

    brought = [
        norm_gain.reshape(1, -1),
        w_read.reshape(1, -1),
        w_value,
        w_query,
        w_key,
        w_gate,
        w_up,
        w_down,
        w_out,
    ]
    sources = pin([cell_order.reshape(1, -1), obs_mask, *brought], pltpu.HBM)
    made = [pltpu.VMEM(array.shape, array.dtype) for k, array in enumerate(brought) if k != 2] + [
        pltpu.VMEM(w_value.shape[::-1], w_value.dtype),
        pltpu.VMEM((1, w_down.shape[0]), jnp.float32),
        pltpu.VMEM((1, w_out.shape[0]), jnp.float32),
        pltpu.VMEM((tile_rows + observables, total), jnp.bfloat16),
        pltpu.VMEM((tile_rows + observables, total), jnp.bfloat16),
        pltpu.VMEM((total, total), jnp.bfloat16),
        pltpu.VMEM((total, total), jnp.float32),
        pltpu.VMEM((observables, LANES), jnp.float32),
    ]
    scratch = [
        pltpu.VMEM((1, cells), jnp.int32),
        pltpu.VMEM(obs_mask.shape, jnp.int32),
        pltpu.VMEM(w_value.shape, w_value.dtype),
        pltpu.SemaphoreType.DMA((len(sources),)),
    ]
    small = pltpu.CompilerParams(vmem_limit_bytes=SMALL_LIMIT)
    preparation = functools.partial(prepare, rounds, cells, len(brought))
    block, *prepared = pl.pallas_call(
        functools.partial(pack_kernel, preparation, len(sources), len(made)),
        out_shape=[pltpu.VMEM((1, cells, width + LANES), jnp.bfloat16), *made],
        in_specs=[hbm] * (len(sources) + 2),
        out_specs=[vmem] * (len(made) + 1),
        scratch_shapes=[
            *scratch,
            pltpu.VMEM(seam_rows.shape[:0:-1], jnp.int32),
            pltpu.VMEM((cells, LANES), jnp.float32),
            pltpu.SemaphoreType.DMA((2,)),
        ],
        compiler_params=small,
    )(*pin([tokens, seam_rows.transpose(0, 2, 1)], pltpu.HBM), *sources)

    def fetch(even, odd):
        pairs = []
        for r in range(rounds):
            for m in range(models):
                shift, flip = odd if m & 1 else even
                pairs.append(((((r - shift) % rounds) ^ flip) * models + m, r * models + m))
        return lax.ppermute(block, ("round", "mp"), pairs)

    def other_core(array):
        return lax.ppermute(array, "mp", [(m, m ^ 1) for m in range(models)])

    direct = [fetch(even, odd) for even, odd in fetch_steps(rounds)]
    prepared = pl.pallas_call(
        functools.partial(late_kernel, preparation, len(sources), len(made)),
        out_shape=made,
        in_specs=[hbm] * len(sources) + [vmem] * len(made),
        out_specs=[vmem] * len(made),
        input_output_aliases={len(sources) + k: k for k in range(len(made))},
        scratch_shapes=scratch,
        compiler_params=small,
        cost_estimate=pl.CostEstimate(flops=0, bytes_accessed=8 * 1024 * 1024, transcendentals=0),
    )(*sources, *pin(prepared, pltpu.VMEM))

    direct[TIED], prepared = lax.optimization_barrier((direct[TIED], prepared))
    blocks = [block]
    for (even, odd), fetched in zip(fetch_steps(rounds), direct):
        blocks += [fetched] if even == odd else [fetched, other_core(fetched)]

    over = pltpu.VMEM((share, width + LANES), jnp.float32)
    stay = pltpu.VMEM((share, width), jnp.float32)
    send_over, send_stay, keep_over, keep_stay = pl.pallas_call(
        functools.partial(layer_kernel, cells, len(blocks)),
        out_shape=(over, stay, over, stay),
        in_specs=[vmem] * (len(blocks) + len(prepared)),
        out_specs=(vmem,) * 4,
        compiler_params=pltpu.CompilerParams(vmem_limit_bytes=LAYER_LIMIT),
    )(*pin([*blocks, *prepared], pltpu.VMEM))
    over = keep_over + other_core(send_over)
    arrived = lax.ppermute(over, "mp", [(m, m ^ 2) for m in range(models)])
    other_stay = other_core(send_stay)
    tiles_out, logits = pl.pallas_call(
        finish_kernel,
        out_shape=(
            jax.ShapeDtypeStruct((share // cell_dev, cell_dev, width), jnp.bfloat16),
            jax.ShapeDtypeStruct((1, observables), jnp.float32),
        ),
        in_specs=[vmem] * 4,
        out_specs=(vmem, vmem),
        compiler_params=pltpu.CompilerParams(vmem_limit_bytes=SMALL_LIMIT),
    )(*pin([over, arrived, keep_stay, other_stay], pltpu.VMEM))
    return tiles_out, logits.reshape(-1)


def fits_whole(mesh, tokens, seam_rows, w_query):
    rounds, models = mesh.shape["round"], mesh.shape["mp"]
    total = tokens.shape[0] * tokens.shape[1]
    share = total // rounds // models
    return (
        models == 4
        and rounds == tokens.shape[0]
        and rounds & (rounds - 1) == 0
        and rounds > 2
        and total <= 512
        and total % LANES == 0
        and total // rounds <= 256
        and share % 8 == 0
        and tokens.shape[1] % 16 == 0
        and seam_rows.shape[2] == 2
        and w_query.shape[1] // models % HDIM == 0
    )


def solution(mesh):
    def layer(*args):
        tokens, seam_rows, w_query = args[0], args[2], args[5]
        whole = fits_whole(mesh, tokens, seam_rows, w_query)
        return placed(mesh, shards_whole if whole else shards_by_tile)(*args)

    return layer


def placed(mesh, shards):
    return jax.shard_map(
        shards,
        mesh=mesh,
        in_specs=(
            P("round", None, None),
            P(),
            P("round", None, None),
            P(),
            P(),
            P(None, "mp"),
            P(None, "mp"),
            P(None, "mp"),
            P("mp", None),
            P(None, "mp"),
            P(None, "mp"),
            P("mp", None),
            P(),
        ),
        out_specs=(P("mp", "round", None), P()),
        check_vma=False,
    )
```

```python
import functools
import math

import jax
import jax.numpy as jnp
from jax import lax
from jax.experimental import pallas as pl
from jax.experimental.pallas import tpu as pltpu
from jax.sharding import PartitionSpec as P

HDIM = 64
LANES = 128
SMALL_LIMIT = 8 * 1024 * 1024
TIED = 0
LAYER_LIMIT = 32 * 1024 * 1024


norm_eps = 1e-06


def normalize(rows_in, norm_gain):
    values = rows_in.astype(jnp.float32)
    spread = jnp.mean(values * values, axis=-1, keepdims=True)
    return (values * lax.rsqrt(spread + norm_eps) * norm_gain).astype(jnp.bfloat16)


def attend(queries, keys_all, values_all, live_keys):
    scale_factor = 1.0 / math.sqrt(queries.shape[-1])
    scores = (
        jnp.einsum("qhe,khe->hqk", queries, keys_all, preferred_element_type=jnp.float32)
        * scale_factor
    )
    if live_keys is not None:
        scores = jnp.where(live_keys[None, None, :], scores, -1e30)
    row_max = jnp.max(scores, axis=-1, keepdims=True)
    weights = jnp.exp(scores - row_max)
    probabilities = (weights / jnp.sum(weights, axis=-1, keepdims=True)).astype(jnp.bfloat16)
    mixture = jnp.einsum(
        "hqk,khe->qhe", probabilities, values_all, preferred_element_type=jnp.float32
    )
    return mixture.reshape(mixture.shape[0], -1)


def shards_by_tile(
    tokens,
    cell_order,
    seam_rows,
    obs_mask,
    norm_gain,
    w_query,
    w_key,
    w_value,
    w_out,
    w_gate,
    w_up,
    w_down,
    w_read,
):
    round_count = lax.axis_size("round")
    model_count = lax.axis_size("mp")
    model_index = lax.axis_index("mp")
    round_index = lax.axis_index("round")
    width = tokens.shape[2]
    cell_dev = tokens.shape[1] // round_count
    permuted = tokens[:, cell_order, :]
    tile_tokens = lax.all_to_all(permuted, "round", split_axis=1, concat_axis=0, tiled=True)
    tile_rows = tile_tokens.shape[0] * cell_dev
    flat_tokens = tile_tokens.reshape(tile_rows, width)
    normed = normalize(flat_tokens, norm_gain)
    queries = jnp.dot(normed, w_query, preferred_element_type=jnp.float32).astype(jnp.bfloat16)
    keys_all = jnp.dot(normed, w_key, preferred_element_type=jnp.float32).astype(jnp.bfloat16)
    values_all = jnp.dot(normed, w_value, preferred_element_type=jnp.float32).astype(jnp.bfloat16)
    head_width = queries.shape[1]
    heads_dev = head_width // HDIM
    block_rows = min(512, tile_rows)
    query_blocks = queries.reshape(tile_rows // block_rows, block_rows, heads_dev, HDIM)
    key_heads = keys_all.reshape(tile_rows, heads_dev, HDIM)
    value_heads = values_all.reshape(tile_rows, heads_dev, HDIM)
    local_attn = lax.map(
        lambda query_block: attend(query_block, key_heads, value_heads, None), query_blocks
    )
    local_attn = local_attn.reshape(tile_rows, head_width)
    live_slot = seam_rows[0] >= 0
    safe_rows = jnp.where(live_slot, seam_rows[0], 0)
    packet = (
        lax.all_to_all(queries[safe_rows], "round", split_axis=0, concat_axis=0, tiled=True),
        lax.all_to_all(keys_all[safe_rows], "round", split_axis=0, concat_axis=0, tiled=True),
        lax.all_to_all(values_all[safe_rows], "round", split_axis=0, concat_axis=0, tiled=True),
        lax.all_to_all(
            live_slot.astype(jnp.bfloat16), "round", split_axis=0, concat_axis=0, tiled=True
        ),
    )
    seam_queries = packet[0].reshape(-1, heads_dev, HDIM)
    seam_keys = packet[1].reshape(-1, heads_dev, HDIM)
    seam_values = packet[2].reshape(-1, heads_dev, HDIM)
    seam_live = packet[3].reshape(-1) > 0.5
    seam_attn = attend(seam_queries, seam_keys, seam_values, seam_live).astype(jnp.bfloat16)
    returned = lax.all_to_all(
        seam_attn.reshape(round_count, -1, head_width),
        "round",
        split_axis=0,
        concat_axis=0,
        tiled=True,
    )
    target = jnp.where(live_slot, seam_rows[0], tile_rows).reshape(-1)
    combined = (
        local_attn.at[target]
        .add(returned.reshape(-1, head_width).astype(jnp.float32), mode="drop")
        .astype(jnp.bfloat16)
    )
    share_rows = tile_rows // model_count
    own_first = model_index * share_rows
    gate_part = jnp.dot(normed, w_gate, preferred_element_type=jnp.float32)
    up_part = jnp.dot(normed, w_up, preferred_element_type=jnp.float32)
    hidden = (jax.nn.silu(gate_part) * up_part).astype(jnp.bfloat16)
    attn_part = jnp.dot(combined, w_out, preferred_element_type=jnp.float32)
    summed = lax.psum_scatter(
        attn_part + jnp.dot(hidden, w_down, preferred_element_type=jnp.float32),
        "mp",
        scatter_dimension=0,
        tiled=True,
    )
    own_rows = lax.dynamic_slice_in_dim(flat_tokens, own_first, share_rows, 0)
    result_rows = (own_rows.astype(jnp.float32) + summed).astype(jnp.bfloat16)
    tiles_out = result_rows.reshape(share_rows // cell_dev, cell_dev, width)
    my_cells = lax.dynamic_slice_in_dim(cell_order, round_index * cell_dev, cell_dev)
    support = obs_mask[:, my_cells].astype(jnp.float32)
    partial_sum = jnp.einsum(
        "oc,rcd->od", support, tiles_out.astype(jnp.float32), precision=lax.Precision.HIGHEST
    )
    support_count = round_count * jnp.sum(obs_mask.astype(jnp.float32), axis=1)
    divisor = jnp.sqrt(support_count)
    pooled = lax.psum(partial_sum, ("round", "mp"))
    obs_logits = jnp.dot(pooled, w_read, precision=lax.Precision.HIGHEST) / divisor
    return (tiles_out, obs_logits)


def iota(shape, dimension):
    return lax.broadcasted_iota(jnp.int32, shape, dimension)


def one_hot(condition):
    return jnp.where(condition, 1.0, 0.0).astype(jnp.bfloat16)


def dot(left, right):
    return jnp.dot(left, right, preferred_element_type=jnp.float32)


def dot_t(left, right):
    return lax.dot_general(
        left, right, (((1,), (1,)), ((), ())), preferred_element_type=jnp.float32
    )


def split_three(values):
    high = values.astype(jnp.bfloat16)
    rest = values - high.astype(jnp.float32)
    middle = rest.astype(jnp.bfloat16)
    low = (rest - middle.astype(jnp.float32)).astype(jnp.bfloat16)
    return jnp.concatenate([high, middle, low], axis=0)


def attend_by_keys(head_vals, scores):
    weights = jnp.exp(scores - jnp.max(scores, axis=0, keepdims=True))
    probabilities = (weights / jnp.sum(weights, axis=0, keepdims=True)).astype(jnp.bfloat16)
    return dot(head_vals, probabilities)


def fetch_steps(rounds):
    shifts = [2, *range(rounds - 2, 2, -2)]
    return [((k, 0), (k, 1)) for k in shifts] + [((0, 1), (0, 1))]


def slot_steps(rounds):
    steps = [((0, 0), (0, 0))]
    for even, odd in fetch_steps(rounds):
        steps += [(even, odd)] if even == odd else [(even, odd), (odd, even)]
    return steps


def pack_kernel(tokens, seam_rows, block, landed, padded, arrivals):
    width = tokens.shape[2]
    slots, owners = seam_rows.shape[1:]
    copies = [
        pltpu.make_async_copy(seam_rows.at[0], landed, arrivals.at[0]),
        pltpu.make_async_copy(tokens, block.at[:, :, :width], arrivals.at[1]),
    ]
    for copy in copies:
        copy.start()
    padded[...] = jnp.zeros(padded.shape, jnp.float32)
    copies[0].wait()
    row = iota((tokens.shape[1], owners), 0)
    held = row == landed[:1]
    for slot in range(1, slots):
        held = held | (row == landed[slot : slot + 1])
    padded[:, :owners] = jnp.where(held, 1.0, 0.0)
    block[0, :, width:] = padded[...].astype(jnp.bfloat16)
    copies[1].wait()


def early_kernel(prepare, *refs):
    @pl.when(lax.axis_index("round") == 0)
    def _():
        prepare(*refs)


def late_kernel(prepare, given, made, *refs):
    @pl.when(lax.axis_index("round") != 0)
    def _():
        prepare(*refs[:given], *refs[given + made :])


def prepare(rounds, cells, counts, *refs):
    order_in, mask_in, *copied = refs[: counts + 2]
    rest = refs[counts + 2 :]
    w_read, w_down, w_out, gain, w_query, w_key, w_gate, w_up = rest[:8]
    w_value_t, read_down, read_out = rest[8:11]
    picks, token_picks, place, tile_bias, divisor = rest[11:16]
    order, mask, w_value, arrivals = rest[16:]
    targets = (order, mask, w_read, w_value, w_down, w_out, gain, w_query, w_key, w_gate, w_up)
    copies = [
        pltpu.make_async_copy(source, target, arrivals.at[k])
        for k, (source, target) in enumerate(zip((order_in, mask_in, *copied), targets))
    ]
    for copy in copies:
        copy.start()
    me, model = lax.axis_index("round"), lax.axis_index("mp")
    core = model & 1
    cell_dev = cells // rounds
    tile_rows = rounds * cell_dev
    share = tile_rows // 4
    total = rounds * cells
    observables = mask.shape[0]

    def slot_round(slot):
        shift, flip = jnp.zeros_like(slot), jnp.zeros_like(slot)
        for k, (even, odd) in enumerate(slot_steps(rounds)):
            shift = jnp.where(slot == k, jnp.where(core == 0, even[0], odd[0]), shift)
            flip = jnp.where(slot == k, jnp.where(core == 0, even[1], odd[1]), flip)
        return ((me + rounds - shift) & (rounds - 1)) ^ flip

    for copy in copies[:2]:
        copy.wait()
    row = iota((total, 1), 0)
    placed = order[...] == lax.rem(row, cells)
    along = iota((1, cells), 1)
    position = jnp.sum(jnp.where(placed, along, 0), axis=1, keepdims=True)
    tile = lax.div(position, cell_dev)
    in_tile = slot_round(lax.div(row, cells)) * cell_dev + lax.rem(position, cell_dev)
    column = iota((1, total), 1)
    slot_start = slot_round(lax.div(column, cells)) * tile_rows
    place[...] = one_hot(tile * tile_rows + in_tile == slot_start + lax.rem(column, cells))
    along_rows = jnp.broadcast_to(along.astype(jnp.float32), (8, cells)).astype(jnp.bfloat16)
    position_row = dot_t(along_rows, one_hot(placed))[:1].astype(jnp.int32)
    tile_row = lax.div(position_row, cell_dev)
    in_tile_row = slot_round(lax.div(column, cells)) * cell_dev + lax.rem(position_row, cell_dev)
    tile_bias[...] = jnp.where(tile == tile_row, 0.0, -1e30)

    index = iota((tile_rows, 1), 0)
    quarter = lax.div(index, share)
    target_model = jnp.where(quarter < 2, model ^ 1, model) ^ jnp.where((quarter & 1) == 0, 3, 0)
    target = target_model * share + lax.rem(index, share)
    own = one_hot((tile_row == me) & (in_tile_row == target))
    mask_bf = mask[...].astype(jnp.float32).astype(jnp.bfloat16)
    support = dot(mask_bf, one_hot(iota((cells, 1), 0) == lax.rem(column, cells))).astype(
        jnp.bfloat16
    )
    picks[:tile_rows] = own
    picks[tile_rows:] = support
    token_picks[:tile_rows] = jnp.where(quarter == 3, own, jnp.zeros_like(own))
    token_picks[tile_rows:] = jnp.where(model == 0, support, jnp.zeros_like(support))
    count = rounds * jnp.sum(mask[...].astype(jnp.float32), axis=1, keepdims=True)
    divisor[...] = jnp.broadcast_to(jnp.sqrt(count), divisor.shape)

    for copy in copies[2:6]:
        copy.wait()
    head_width = w_value.shape[1]
    identity = one_hot(iota((head_width, 1), 0) == iota((1, head_width), 1))
    w_value_t[...] = dot_t(identity, w_value[...]).astype(jnp.bfloat16)
    read_parts = split_three(jnp.broadcast_to(w_read[...], (8, w_read.shape[1])))
    for weight, read in ((w_down, read_down), (w_out, read_out)):
        parts = dot_t(read_parts, weight[...])
        read[...] = parts[:1] + parts[8:9] + parts[16:17]
    for copy in copies[6:]:
        copy.wait()


def layer_kernel(cells, slots, *refs):
    blocks, rest = refs[:slots], refs[slots:]
    w_read, w_down, w_out, gain, w_query, w_key, w_gate, w_up = rest[:8]
    w_value_t, read_down, read_out = rest[8:11]
    picks, token_picks, place, tile_bias, divisor = rest[11:16]
    outs = rest[16:]
    total = slots * cells
    width = gain.shape[1]
    head_width = w_query.shape[1]
    observables = divisor.shape[0]
    tile_rows = picks.shape[0] - observables

    tokens = jnp.concatenate([block[0, :, :width] for block in blocks], axis=0)
    token_rows = dot(token_picks[...], tokens)

    members = jnp.concatenate([block[0, :, width:] for block in blocks], axis=0)
    member = dot(place[...], members).astype(jnp.bfloat16)

    values = tokens.astype(jnp.float32)
    spread = jnp.mean(values * values, axis=-1, keepdims=True)
    normed = (values * lax.rsqrt(spread + norm_eps) * gain[...]).astype(jnp.bfloat16)

    queries = (dot(normed, w_query[...]) * (1.0 / math.sqrt(HDIM))).astype(jnp.bfloat16)
    keys = dot(normed, w_key[...]).astype(jnp.bfloat16)
    vals = dot_t(w_value_t[...], normed).astype(jnp.bfloat16)

    gate = dot(normed, w_gate[...])
    up = dot(normed, w_up[...])
    hidden = (gate / (1.0 + jnp.exp(-gate)) * up).astype(jnp.bfloat16)

    seam_bias = jnp.where(dot_t(member, member) > 0.5, 0.0, -1e30)
    in_seam = dot_t(jnp.ones((8, LANES), jnp.bfloat16), member)[:1] > 0.5
    lane_head = lax.div(iota((1, head_width), 1), HDIM)
    parts = []
    for first in range(0, total, LANES):
        some = slice(first, first + LANES)
        mixed = []
        for head in range(head_width // HDIM):
            head_keys = jnp.where(lane_head == head, keys, jnp.zeros_like(keys))
            head_vals = vals[head * HDIM : (head + 1) * HDIM]
            scores = dot_t(head_keys, queries[some])
            local = attend_by_keys(head_vals, scores + tile_bias[:, some])
            seam = attend_by_keys(head_vals, scores + seam_bias[:, some])
            seam = seam.astype(jnp.bfloat16).astype(jnp.float32)
            mixed.append((local + jnp.where(in_seam[:, some], seam, 0.0)).astype(jnp.bfloat16))
        parts.append(jnp.concatenate(mixed, axis=0))
    combined = jnp.concatenate(parts, axis=1)

    hidden_rows = dot(picks[...], hidden)
    combined_rows = dot_t(picks[...], combined)
    update = (
        token_rows[:tile_rows]
        + dot(hidden_rows[:tile_rows].astype(jnp.bfloat16), w_down[...])
        + dot(combined_rows[:tile_rows].astype(jnp.bfloat16), w_out[...])
    )
    logits = sum(
        jnp.sum(sums[tile_rows:] * read[...], axis=1, keepdims=True)
        for sums, read in (
            (hidden_rows, read_down),
            (combined_rows, read_out),
            (token_rows, w_read),
        )
    )
    logits = logits / divisor[:, :1]
    diagonal = iota((observables, LANES), 0) == iota((observables, LANES), 1)
    logits_row = jnp.sum(jnp.where(diagonal, logits, 0.0), axis=0, keepdims=True)
    share = tile_rows // 4
    send_over, send_stay, keep_over, keep_stay = outs
    for k, (over, stay) in enumerate(((send_over, send_stay), (keep_over, keep_stay))):
        over[:, :width] = update[2 * k * share : (2 * k + 1) * share]
        over[:, width:] = jnp.broadcast_to(logits_row, (share, LANES))
        stay[...] = update[(2 * k + 1) * share : (2 * k + 2) * share]


def finish_kernel(over, arrived, stay, other_stay, tiles_out, logits_out):
    count, cell_dev = tiles_out.shape[:2]
    width = stay.shape[1]
    rows = stay[...] + other_stay[...] + arrived[:, :width]
    for k in range(count):
        tiles_out[k] = rows[k * cell_dev : (k + 1) * cell_dev].astype(tiles_out.dtype)
    logits = over[:1, width:] + arrived[:1, width:]
    logits_out[...] = logits[:, : logits_out.shape[1]]


def shards_whole(
    tokens,
    cell_order,
    seam_rows,
    obs_mask,
    norm_gain,
    w_query,
    w_key,
    w_value,
    w_out,
    w_gate,
    w_up,
    w_down,
    w_read,
):
    rounds = lax.axis_size("round")
    models = lax.axis_size("mp")
    cells, width = tokens.shape[1:]
    cell_dev = cells // rounds
    tile_rows = rounds * cell_dev
    share = tile_rows // models
    total = rounds * cells
    observables = obs_mask.shape[0]
    vmem = pl.BlockSpec(memory_space=pltpu.VMEM)
    hbm = pl.BlockSpec(memory_space=pltpu.HBM)

    def pin(arrays, space):
        return [pltpu.with_memory_space_constraint(array, space) for array in arrays]

    brought = [
        w_read.reshape(1, -1),
        w_value,
        w_down,
        w_out,
        norm_gain.reshape(1, -1),
        w_query,
        w_key,
        w_gate,
        w_up,
    ]
    sources = pin([cell_order.reshape(1, -1), obs_mask, *brought], pltpu.HBM)
    made = [pltpu.VMEM(array.shape, array.dtype) for array in brought if array is not w_value] + [
        pltpu.VMEM(w_value.shape[::-1], w_value.dtype),
        pltpu.VMEM((1, w_down.shape[0]), jnp.float32),
        pltpu.VMEM((1, w_out.shape[0]), jnp.float32),
        pltpu.VMEM((tile_rows + observables, total), jnp.bfloat16),
        pltpu.VMEM((tile_rows + observables, total), jnp.bfloat16),
        pltpu.VMEM((total, total), jnp.bfloat16),
        pltpu.VMEM((total, total), jnp.float32),
        pltpu.VMEM((observables, LANES), jnp.float32),
    ]
    scratch = [
        pltpu.VMEM((1, cells), jnp.int32),
        pltpu.VMEM(obs_mask.shape, jnp.int32),
        pltpu.VMEM(w_value.shape, w_value.dtype),
        pltpu.SemaphoreType.DMA((len(sources),)),
    ]
    small = pltpu.CompilerParams(vmem_limit_bytes=SMALL_LIMIT)
    preparation = functools.partial(prepare, rounds, cells, len(brought))
    block = pl.pallas_call(
        pack_kernel,
        out_shape=pltpu.VMEM((1, cells, width + LANES), jnp.bfloat16),
        in_specs=[hbm, hbm],
        out_specs=vmem,
        scratch_shapes=[
            pltpu.VMEM(seam_rows.shape[:0:-1], jnp.int32),
            pltpu.VMEM((cells, LANES), jnp.float32),
            pltpu.SemaphoreType.DMA((2,)),
        ],
        compiler_params=small,
    )(*pin([tokens, seam_rows.transpose(0, 2, 1)], pltpu.HBM))
    prepared = pl.pallas_call(
        functools.partial(early_kernel, preparation),
        out_shape=made,
        in_specs=[hbm] * len(sources),
        out_specs=[vmem] * len(made),
        scratch_shapes=scratch,
        compiler_params=small,
    )(*sources)
    block, prepared = lax.optimization_barrier((block, prepared))

    def fetch(even, odd):
        pairs = []
        for r in range(rounds):
            for m in range(models):
                shift, flip = odd if m & 1 else even
                pairs.append(((((r - shift) % rounds) ^ flip) * models + m, r * models + m))
        return lax.ppermute(block, ("round", "mp"), pairs)

    def other_core(array):
        return lax.ppermute(array, "mp", [(m, m ^ 1) for m in range(models)])

    direct = [fetch(even, odd) for even, odd in fetch_steps(rounds)]
    prepared = pl.pallas_call(
        functools.partial(late_kernel, preparation, len(sources), len(made)),
        out_shape=made,
        in_specs=[hbm] * len(sources) + [vmem] * len(made),
        out_specs=[vmem] * len(made),
        input_output_aliases={len(sources) + k: k for k in range(len(made))},
        scratch_shapes=scratch,
        compiler_params=small,
        cost_estimate=pl.CostEstimate(flops=0, bytes_accessed=8 * 1024 * 1024, transcendentals=0),
    )(*sources, *pin(prepared, pltpu.VMEM))

    direct[TIED], prepared = lax.optimization_barrier((direct[TIED], prepared))
    blocks = [block]
    for (even, odd), fetched in zip(fetch_steps(rounds), direct):
        blocks += [fetched] if even == odd else [fetched, other_core(fetched)]

    over = pltpu.VMEM((share, width + LANES), jnp.float32)
    stay = pltpu.VMEM((share, width), jnp.float32)
    send_over, send_stay, keep_over, keep_stay = pl.pallas_call(
        functools.partial(layer_kernel, cells, len(blocks)),
        out_shape=(over, stay, over, stay),
        in_specs=[vmem] * (len(blocks) + len(prepared)),
        out_specs=(vmem,) * 4,
        compiler_params=pltpu.CompilerParams(vmem_limit_bytes=LAYER_LIMIT),
    )(*pin([*blocks, *prepared], pltpu.VMEM))
    over = keep_over + other_core(send_over)
    arrived = lax.ppermute(over, "mp", [(m, m ^ 3) for m in range(models)])
    other_stay = other_core(send_stay)
    tiles_out, logits = pl.pallas_call(
        finish_kernel,
        out_shape=(
            jax.ShapeDtypeStruct((share // cell_dev, cell_dev, width), jnp.bfloat16),
            jax.ShapeDtypeStruct((1, observables), jnp.float32),
        ),
        in_specs=[vmem] * 4,
        out_specs=(vmem, vmem),
        compiler_params=pltpu.CompilerParams(vmem_limit_bytes=SMALL_LIMIT),
    )(*pin([over, arrived, keep_stay, other_stay], pltpu.VMEM))
    return tiles_out, logits.reshape(-1)


def fits_whole(mesh, tokens, seam_rows, w_query):
    rounds, models = mesh.shape["round"], mesh.shape["mp"]
    total = tokens.shape[0] * tokens.shape[1]
    share = total // rounds // models
    return (
        models == 4
        and rounds == tokens.shape[0]
        and rounds & (rounds - 1) == 0
        and rounds > 2
        and total <= 512
        and total % LANES == 0
        and total // rounds <= 256
        and share % 8 == 0
        and tokens.shape[1] % 16 == 0
        and seam_rows.shape[2] == 2
        and w_query.shape[1] // models % HDIM == 0
    )


def solution(mesh):
    def layer(*args):
        tokens, seam_rows, w_query = args[0], args[2], args[5]
        whole = fits_whole(mesh, tokens, seam_rows, w_query)
        return placed(mesh, shards_whole if whole else shards_by_tile)(*args)

    return layer


def placed(mesh, shards):
    return jax.shard_map(
        shards,
        mesh=mesh,
        in_specs=(
            P("round", None, None),
            P(),
            P("round", None, None),
            P(),
            P(),
            P(None, "mp"),
            P(None, "mp"),
            P(None, "mp"),
            P("mp", None),
            P(None, "mp"),
            P(None, "mp"),
            P("mp", None),
            P(),
        ),
        out_specs=(P("mp", "round", None), P()),
        check_vma=False,
    )
```

```python
import functools
import math

import jax
import jax.numpy as jnp
from jax import lax
from jax.experimental import pallas as pl
from jax.experimental.pallas import tpu as pltpu
from jax.sharding import PartitionSpec as P

HDIM = 64
LANES = 128
SMALL_LIMIT = 8 * 1024 * 1024
LAYER_LIMIT = 32 * 1024 * 1024


norm_eps = 1e-06


def normalize(rows_in, norm_gain):
    values = rows_in.astype(jnp.float32)
    spread = jnp.mean(values * values, axis=-1, keepdims=True)
    return (values * lax.rsqrt(spread + norm_eps) * norm_gain).astype(jnp.bfloat16)


def attend(queries, keys_all, values_all, live_keys):
    scale_factor = 1.0 / math.sqrt(queries.shape[-1])
    scores = (
        jnp.einsum("qhe,khe->hqk", queries, keys_all, preferred_element_type=jnp.float32)
        * scale_factor
    )
    if live_keys is not None:
        scores = jnp.where(live_keys[None, None, :], scores, -1e30)
    row_max = jnp.max(scores, axis=-1, keepdims=True)
    weights = jnp.exp(scores - row_max)
    probabilities = (weights / jnp.sum(weights, axis=-1, keepdims=True)).astype(jnp.bfloat16)
    mixture = jnp.einsum(
        "hqk,khe->qhe", probabilities, values_all, preferred_element_type=jnp.float32
    )
    return mixture.reshape(mixture.shape[0], -1)


def shards_by_tile(
    tokens,
    cell_order,
    seam_rows,
    obs_mask,
    norm_gain,
    w_query,
    w_key,
    w_value,
    w_out,
    w_gate,
    w_up,
    w_down,
    w_read,
):
    round_count = lax.axis_size("round")
    model_count = lax.axis_size("mp")
    model_index = lax.axis_index("mp")
    round_index = lax.axis_index("round")
    width = tokens.shape[2]
    cell_dev = tokens.shape[1] // round_count
    permuted = tokens[:, cell_order, :]
    tile_tokens = lax.all_to_all(permuted, "round", split_axis=1, concat_axis=0, tiled=True)
    tile_rows = tile_tokens.shape[0] * cell_dev
    flat_tokens = tile_tokens.reshape(tile_rows, width)
    normed = normalize(flat_tokens, norm_gain)
    queries = jnp.dot(normed, w_query, preferred_element_type=jnp.float32).astype(jnp.bfloat16)
    keys_all = jnp.dot(normed, w_key, preferred_element_type=jnp.float32).astype(jnp.bfloat16)
    values_all = jnp.dot(normed, w_value, preferred_element_type=jnp.float32).astype(jnp.bfloat16)
    head_width = queries.shape[1]
    heads_dev = head_width // HDIM
    block_rows = min(512, tile_rows)
    query_blocks = queries.reshape(tile_rows // block_rows, block_rows, heads_dev, HDIM)
    key_heads = keys_all.reshape(tile_rows, heads_dev, HDIM)
    value_heads = values_all.reshape(tile_rows, heads_dev, HDIM)
    local_attn = lax.map(
        lambda query_block: attend(query_block, key_heads, value_heads, None), query_blocks
    )
    local_attn = local_attn.reshape(tile_rows, head_width)
    live_slot = seam_rows[0] >= 0
    safe_rows = jnp.where(live_slot, seam_rows[0], 0)
    packet = (
        lax.all_to_all(queries[safe_rows], "round", split_axis=0, concat_axis=0, tiled=True),
        lax.all_to_all(keys_all[safe_rows], "round", split_axis=0, concat_axis=0, tiled=True),
        lax.all_to_all(values_all[safe_rows], "round", split_axis=0, concat_axis=0, tiled=True),
        lax.all_to_all(
            live_slot.astype(jnp.bfloat16), "round", split_axis=0, concat_axis=0, tiled=True
        ),
    )
    seam_queries = packet[0].reshape(-1, heads_dev, HDIM)
    seam_keys = packet[1].reshape(-1, heads_dev, HDIM)
    seam_values = packet[2].reshape(-1, heads_dev, HDIM)
    seam_live = packet[3].reshape(-1) > 0.5
    seam_attn = attend(seam_queries, seam_keys, seam_values, seam_live).astype(jnp.bfloat16)
    returned = lax.all_to_all(
        seam_attn.reshape(round_count, -1, head_width),
        "round",
        split_axis=0,
        concat_axis=0,
        tiled=True,
    )
    target = jnp.where(live_slot, seam_rows[0], tile_rows).reshape(-1)
    combined = (
        local_attn.at[target]
        .add(returned.reshape(-1, head_width).astype(jnp.float32), mode="drop")
        .astype(jnp.bfloat16)
    )
    share_rows = tile_rows // model_count
    own_first = model_index * share_rows
    gate_part = jnp.dot(normed, w_gate, preferred_element_type=jnp.float32)
    up_part = jnp.dot(normed, w_up, preferred_element_type=jnp.float32)
    hidden = (jax.nn.silu(gate_part) * up_part).astype(jnp.bfloat16)
    attn_part = jnp.dot(combined, w_out, preferred_element_type=jnp.float32)
    summed = lax.psum_scatter(
        attn_part + jnp.dot(hidden, w_down, preferred_element_type=jnp.float32),
        "mp",
        scatter_dimension=0,
        tiled=True,
    )
    own_rows = lax.dynamic_slice_in_dim(flat_tokens, own_first, share_rows, 0)
    result_rows = (own_rows.astype(jnp.float32) + summed).astype(jnp.bfloat16)
    tiles_out = result_rows.reshape(share_rows // cell_dev, cell_dev, width)
    my_cells = lax.dynamic_slice_in_dim(cell_order, round_index * cell_dev, cell_dev)
    support = obs_mask[:, my_cells].astype(jnp.float32)
    partial_sum = jnp.einsum(
        "oc,rcd->od", support, tiles_out.astype(jnp.float32), precision=lax.Precision.HIGHEST
    )
    support_count = round_count * jnp.sum(obs_mask.astype(jnp.float32), axis=1)
    divisor = jnp.sqrt(support_count)
    pooled = lax.psum(partial_sum, ("round", "mp"))
    obs_logits = jnp.dot(pooled, w_read, precision=lax.Precision.HIGHEST) / divisor
    return (tiles_out, obs_logits)


def iota(shape, dimension):
    return lax.broadcasted_iota(jnp.int32, shape, dimension)


def one_hot(condition):
    return jnp.where(condition, 1.0, 0.0).astype(jnp.bfloat16)


def dot(left, right):
    return jnp.dot(left, right, preferred_element_type=jnp.float32)


def dot_t(left, right):
    return lax.dot_general(
        left, right, (((1,), (1,)), ((), ())), preferred_element_type=jnp.float32
    )


def split_three(values):
    high = values.astype(jnp.bfloat16)
    rest = values - high.astype(jnp.float32)
    middle = rest.astype(jnp.bfloat16)
    low = (rest - middle.astype(jnp.float32)).astype(jnp.bfloat16)
    return jnp.concatenate([high, middle, low], axis=0)


def attend_by_keys(head_vals, scores):
    weights = jnp.exp(scores - jnp.max(scores, axis=0, keepdims=True))
    probabilities = (weights / jnp.sum(weights, axis=0, keepdims=True)).astype(jnp.bfloat16)
    return dot(head_vals, probabilities)


def fetch_steps(rounds):
    return [((k, 0), (k, 1)) for k in range(rounds - 2, 0, -2)] + [((0, 1), (0, 1))]


def slot_steps(rounds):
    steps = [((0, 0), (0, 0))]
    for even, odd in fetch_steps(rounds):
        steps += [(even, odd)] if even == odd else [(even, odd), (odd, even)]
    return steps


def pack_kernel(tokens, seam_rows, block, landed, padded, arrivals):
    width = tokens.shape[2]
    slots, owners = seam_rows.shape[1:]
    copies = [
        pltpu.make_async_copy(seam_rows.at[0], landed, arrivals.at[0]),
        pltpu.make_async_copy(tokens, block.at[:, :, :width], arrivals.at[1]),
    ]
    for copy in copies:
        copy.start()
    padded[...] = jnp.zeros(padded.shape, jnp.float32)
    copies[0].wait()
    row = iota((tokens.shape[1], owners), 0)
    held = row == landed[:1]
    for slot in range(1, slots):
        held = held | (row == landed[slot : slot + 1])
    padded[:, :owners] = jnp.where(held, 1.0, 0.0)
    block[0, :, width:] = padded[...].astype(jnp.bfloat16)
    copies[1].wait()


def early_kernel(prepare, *refs):
    @pl.when(lax.axis_index("round") == 0)
    def _():
        prepare(*refs)


def late_kernel(prepare, given, made, *refs):
    @pl.when(lax.axis_index("round") != 0)
    def _():
        prepare(*refs[:given], *refs[given + made :])


def prepare(rounds, cells, counts, *refs):
    order_in, mask_in, *copied = refs[: counts + 2]
    rest = refs[counts + 2 :]
    w_read, w_down, w_out, gain, w_query, w_key, w_gate, w_up = rest[:8]
    w_value_t, read_down, read_out = rest[8:11]
    picks, token_picks, place, tile_bias, divisor = rest[11:16]
    order, mask, w_value, arrivals = rest[16:]
    targets = (order, mask, w_read, w_value, w_down, w_out, gain, w_query, w_key, w_gate, w_up)
    copies = [
        pltpu.make_async_copy(source, target, arrivals.at[k])
        for k, (source, target) in enumerate(zip((order_in, mask_in, *copied), targets))
    ]
    for copy in copies:
        copy.start()
    me, model = lax.axis_index("round"), lax.axis_index("mp")
    core = model & 1
    cell_dev = cells // rounds
    tile_rows = rounds * cell_dev
    share = tile_rows // 4
    total = rounds * cells
    observables = mask.shape[0]

    def slot_round(slot):
        shift, flip = jnp.zeros_like(slot), jnp.zeros_like(slot)
        for k, (even, odd) in enumerate(slot_steps(rounds)):
            shift = jnp.where(slot == k, jnp.where(core == 0, even[0], odd[0]), shift)
            flip = jnp.where(slot == k, jnp.where(core == 0, even[1], odd[1]), flip)
        return ((me + rounds - shift) & (rounds - 1)) ^ flip

    for copy in copies[:2]:
        copy.wait()
    row = iota((total, 1), 0)
    placed = order[...] == lax.rem(row, cells)
    along = iota((1, cells), 1)
    position = jnp.sum(jnp.where(placed, along, 0), axis=1, keepdims=True)
    tile = lax.div(position, cell_dev)
    in_tile = slot_round(lax.div(row, cells)) * cell_dev + lax.rem(position, cell_dev)
    column = iota((1, total), 1)
    slot_start = slot_round(lax.div(column, cells)) * tile_rows
    place[...] = one_hot(tile * tile_rows + in_tile == slot_start + lax.rem(column, cells))
    along_rows = jnp.broadcast_to(along.astype(jnp.float32), (8, cells)).astype(jnp.bfloat16)
    position_row = dot_t(along_rows, one_hot(placed))[:1].astype(jnp.int32)
    tile_row = lax.div(position_row, cell_dev)
    in_tile_row = slot_round(lax.div(column, cells)) * cell_dev + lax.rem(position_row, cell_dev)
    tile_bias[...] = jnp.where(tile == tile_row, 0.0, -1e30)

    index = iota((tile_rows, 1), 0)
    quarter = lax.div(index, share)
    target_model = jnp.where(quarter < 2, model ^ 1, model) ^ jnp.where((quarter & 1) == 0, 3, 0)
    target = target_model * share + lax.rem(index, share)
    own = one_hot((tile_row == me) & (in_tile_row == target))
    mask_bf = mask[...].astype(jnp.float32).astype(jnp.bfloat16)
    support = dot(mask_bf, one_hot(iota((cells, 1), 0) == lax.rem(column, cells))).astype(
        jnp.bfloat16
    )
    picks[:tile_rows] = own
    picks[tile_rows:] = support
    token_picks[:tile_rows] = jnp.where(quarter == 3, own, jnp.zeros_like(own))
    token_picks[tile_rows:] = jnp.where(model == 0, support, jnp.zeros_like(support))
    count = rounds * jnp.sum(mask[...].astype(jnp.float32), axis=1, keepdims=True)
    divisor[...] = jnp.broadcast_to(jnp.sqrt(count), divisor.shape)

    for copy in copies[2:6]:
        copy.wait()
    head_width = w_value.shape[1]
    identity = one_hot(iota((head_width, 1), 0) == iota((1, head_width), 1))
    w_value_t[...] = dot_t(identity, w_value[...]).astype(jnp.bfloat16)
    read_parts = split_three(jnp.broadcast_to(w_read[...], (8, w_read.shape[1])))
    for weight, read in ((w_down, read_down), (w_out, read_out)):
        parts = dot_t(read_parts, weight[...])
        read[...] = parts[:1] + parts[8:9] + parts[16:17]
    for copy in copies[6:]:
        copy.wait()


def layer_kernel(cells, slots, *refs):
    blocks, rest = refs[:slots], refs[slots:]
    w_read, w_down, w_out, gain, w_query, w_key, w_gate, w_up = rest[:8]
    w_value_t, read_down, read_out = rest[8:11]
    picks, token_picks, place, tile_bias, divisor = rest[11:16]
    outs = rest[16:]
    total = slots * cells
    width = gain.shape[1]
    head_width = w_query.shape[1]
    observables = divisor.shape[0]
    tile_rows = picks.shape[0] - observables

    tokens = jnp.concatenate([block[0, :, :width] for block in blocks], axis=0)
    token_rows = dot(token_picks[...], tokens)

    members = jnp.concatenate([block[0, :, width:] for block in blocks], axis=0)
    member = dot(place[...], members).astype(jnp.bfloat16)

    values = tokens.astype(jnp.float32)
    spread = jnp.mean(values * values, axis=-1, keepdims=True)
    normed = (values * lax.rsqrt(spread + norm_eps) * gain[...]).astype(jnp.bfloat16)

    queries = (dot(normed, w_query[...]) * (1.0 / math.sqrt(HDIM))).astype(jnp.bfloat16)
    keys = dot(normed, w_key[...]).astype(jnp.bfloat16)
    vals = dot_t(w_value_t[...], normed).astype(jnp.bfloat16)

    gate = dot(normed, w_gate[...])
    up = dot(normed, w_up[...])
    hidden = (gate / (1.0 + jnp.exp(-gate)) * up).astype(jnp.bfloat16)

    seam_bias = jnp.where(dot_t(member, member) > 0.5, 0.0, -1e30)
    in_seam = dot_t(jnp.ones((8, LANES), jnp.bfloat16), member)[:1] > 0.5
    lane_head = lax.div(iota((1, head_width), 1), HDIM)
    parts = []
    for first in range(0, total, LANES):
        some = slice(first, first + LANES)
        mixed = []
        for head in range(head_width // HDIM):
            head_keys = jnp.where(lane_head == head, keys, jnp.zeros_like(keys))
            head_vals = vals[head * HDIM : (head + 1) * HDIM]
            scores = dot_t(head_keys, queries[some])
            local = attend_by_keys(head_vals, scores + tile_bias[:, some])
            seam = attend_by_keys(head_vals, scores + seam_bias[:, some])
            seam = seam.astype(jnp.bfloat16).astype(jnp.float32)
            mixed.append((local + jnp.where(in_seam[:, some], seam, 0.0)).astype(jnp.bfloat16))
        parts.append(jnp.concatenate(mixed, axis=0))
    combined = jnp.concatenate(parts, axis=1)

    hidden_rows = dot(picks[...], hidden)
    combined_rows = dot_t(picks[...], combined)
    update = (
        token_rows[:tile_rows]
        + dot(hidden_rows[:tile_rows].astype(jnp.bfloat16), w_down[...])
        + dot(combined_rows[:tile_rows].astype(jnp.bfloat16), w_out[...])
    )
    logits = sum(
        jnp.sum(sums[tile_rows:] * read[...], axis=1, keepdims=True)
        for sums, read in (
            (hidden_rows, read_down),
            (combined_rows, read_out),
            (token_rows, w_read),
        )
    )
    logits = logits / divisor[:, :1]
    diagonal = iota((observables, LANES), 0) == iota((observables, LANES), 1)
    logits_row = jnp.sum(jnp.where(diagonal, logits, 0.0), axis=0, keepdims=True)
    share = tile_rows // 4
    send_over, send_stay, keep_over, keep_stay = outs
    for k, (over, stay) in enumerate(((send_over, send_stay), (keep_over, keep_stay))):
        over[:, :width] = update[2 * k * share : (2 * k + 1) * share]
        over[:, width:] = jnp.broadcast_to(logits_row, (share, LANES))
        stay[...] = update[(2 * k + 1) * share : (2 * k + 2) * share]


def finish_kernel(over, arrived, stay, other_stay, tiles_out, logits_out):
    count, cell_dev = tiles_out.shape[:2]
    width = stay.shape[1]
    rows = stay[...] + other_stay[...] + arrived[:, :width]
    for k in range(count):
        tiles_out[k] = rows[k * cell_dev : (k + 1) * cell_dev].astype(tiles_out.dtype)
    logits = over[:1, width:] + arrived[:1, width:]
    logits_out[...] = logits[:, : logits_out.shape[1]]


def shards_whole(
    tokens,
    cell_order,
    seam_rows,
    obs_mask,
    norm_gain,
    w_query,
    w_key,
    w_value,
    w_out,
    w_gate,
    w_up,
    w_down,
    w_read,
):
    rounds = lax.axis_size("round")
    models = lax.axis_size("mp")
    cells, width = tokens.shape[1:]
    cell_dev = cells // rounds
    tile_rows = rounds * cell_dev
    share = tile_rows // models
    total = rounds * cells
    observables = obs_mask.shape[0]
    vmem = pl.BlockSpec(memory_space=pltpu.VMEM)
    hbm = pl.BlockSpec(memory_space=pltpu.HBM)

    def pin(arrays, space):
        return [pltpu.with_memory_space_constraint(array, space) for array in arrays]

    brought = [
        w_read.reshape(1, -1),
        w_value,
        w_down,
        w_out,
        norm_gain.reshape(1, -1),
        w_query,
        w_key,
        w_gate,
        w_up,
    ]
    sources = pin([cell_order.reshape(1, -1), obs_mask, *brought], pltpu.HBM)
    made = [pltpu.VMEM(array.shape, array.dtype) for array in brought if array is not w_value] + [
        pltpu.VMEM(w_value.shape[::-1], w_value.dtype),
        pltpu.VMEM((1, w_down.shape[0]), jnp.float32),
        pltpu.VMEM((1, w_out.shape[0]), jnp.float32),
        pltpu.VMEM((tile_rows + observables, total), jnp.bfloat16),
        pltpu.VMEM((tile_rows + observables, total), jnp.bfloat16),
        pltpu.VMEM((total, total), jnp.bfloat16),
        pltpu.VMEM((total, total), jnp.float32),
        pltpu.VMEM((observables, LANES), jnp.float32),
    ]
    scratch = [
        pltpu.VMEM((1, cells), jnp.int32),
        pltpu.VMEM(obs_mask.shape, jnp.int32),
        pltpu.VMEM(w_value.shape, w_value.dtype),
        pltpu.SemaphoreType.DMA((len(sources),)),
    ]
    small = pltpu.CompilerParams(vmem_limit_bytes=SMALL_LIMIT)
    preparation = functools.partial(prepare, rounds, cells, len(brought))
    block = pl.pallas_call(
        pack_kernel,
        out_shape=pltpu.VMEM((1, cells, width + LANES), jnp.bfloat16),
        in_specs=[hbm, hbm],
        out_specs=vmem,
        scratch_shapes=[
            pltpu.VMEM(seam_rows.shape[:0:-1], jnp.int32),
            pltpu.VMEM((cells, LANES), jnp.float32),
            pltpu.SemaphoreType.DMA((2,)),
        ],
        compiler_params=small,
    )(*pin([tokens, seam_rows.transpose(0, 2, 1)], pltpu.HBM))
    prepared = pl.pallas_call(
        functools.partial(early_kernel, preparation),
        out_shape=made,
        in_specs=[hbm] * len(sources),
        out_specs=[vmem] * len(made),
        scratch_shapes=scratch,
        compiler_params=small,
    )(*sources)
    block, prepared = lax.optimization_barrier((block, prepared))

    def fetch(even, odd):
        across = 1 if even == odd else 0
        pairs = []
        for r in range(rounds):
            for m in range(models):
                shift, flip = odd if m & 1 else even
                source = ((r - shift) % rounds) ^ flip
                pairs.append((source * models + (m ^ across), r * models + m))
        return lax.ppermute(block, ("round", "mp"), pairs)

    def other_core(array):
        return lax.ppermute(array, "mp", [(m, m ^ 1) for m in range(models)])

    direct = [fetch(even, odd) for even, odd in fetch_steps(rounds)]
    prepared = pl.pallas_call(
        functools.partial(late_kernel, preparation, len(sources), len(made)),
        out_shape=made,
        in_specs=[hbm] * len(sources) + [vmem] * len(made),
        out_specs=[vmem] * len(made),
        input_output_aliases={len(sources) + k: k for k in range(len(made))},
        scratch_shapes=scratch,
        compiler_params=small,
        cost_estimate=pl.CostEstimate(flops=0, bytes_accessed=8 * 1024 * 1024, transcendentals=0),
    )(*sources, *pin(prepared, pltpu.VMEM))

    direct[-2], prepared = lax.optimization_barrier((direct[-2], prepared))
    blocks = [block]
    for (even, odd), fetched in zip(fetch_steps(rounds), direct):
        blocks += [fetched] if even == odd else [fetched, other_core(fetched)]

    over = pltpu.VMEM((share, width + LANES), jnp.float32)
    stay = pltpu.VMEM((share, width), jnp.float32)
    send_over, send_stay, keep_over, keep_stay = pl.pallas_call(
        functools.partial(layer_kernel, cells, len(blocks)),
        out_shape=(over, stay, over, stay),
        in_specs=[vmem] * (len(blocks) + len(prepared)),
        out_specs=(vmem,) * 4,
        compiler_params=pltpu.CompilerParams(vmem_limit_bytes=LAYER_LIMIT),
    )(*pin([*blocks, *prepared], pltpu.VMEM))
    over = keep_over + other_core(send_over)
    arrived = lax.ppermute(over, "mp", [(m, m ^ 3) for m in range(models)])
    other_stay = other_core(send_stay)
    tiles_out, logits = pl.pallas_call(
        finish_kernel,
        out_shape=(
            jax.ShapeDtypeStruct((share // cell_dev, cell_dev, width), jnp.bfloat16),
            jax.ShapeDtypeStruct((1, observables), jnp.float32),
        ),
        in_specs=[vmem] * 4,
        out_specs=(vmem, vmem),
        compiler_params=pltpu.CompilerParams(vmem_limit_bytes=SMALL_LIMIT),
    )(*pin([over, arrived, keep_stay, other_stay], pltpu.VMEM))
    return tiles_out, logits.reshape(-1)


def fits_whole(mesh, tokens, seam_rows, w_query):
    rounds, models = mesh.shape["round"], mesh.shape["mp"]
    total = tokens.shape[0] * tokens.shape[1]
    share = total // rounds // models
    return (
        models == 4
        and rounds == tokens.shape[0]
        and rounds & (rounds - 1) == 0
        and rounds > 2
        and total <= 512
        and total % LANES == 0
        and total // rounds <= 256
        and share % 8 == 0
        and tokens.shape[1] % 16 == 0
        and seam_rows.shape[2] == 2
        and w_query.shape[1] // models % HDIM == 0
    )


def solution(mesh):
    def layer(*args):
        tokens, seam_rows, w_query = args[0], args[2], args[5]
        whole = fits_whole(mesh, tokens, seam_rows, w_query)
        return placed(mesh, shards_whole if whole else shards_by_tile)(*args)

    return layer


def placed(mesh, shards):
    return jax.shard_map(
        shards,
        mesh=mesh,
        in_specs=(
            P("round", None, None),
            P(),
            P("round", None, None),
            P(),
            P(),
            P(None, "mp"),
            P(None, "mp"),
            P(None, "mp"),
            P("mp", None),
            P(None, "mp"),
            P(None, "mp"),
            P("mp", None),
            P(),
        ),
        out_specs=(P("mp", "round", None), P()),
        check_vma=False,
    )
```

```python
import functools
import math

import jax
import jax.numpy as jnp
from jax import lax
from jax.experimental import pallas as pl
from jax.experimental.pallas import tpu as pltpu
from jax.sharding import PartitionSpec as P

HDIM = 64
LANES = 128
SMALL_LIMIT = 8 * 1024 * 1024
LAYER_LIMIT = 32 * 1024 * 1024


norm_eps = 1e-06


def normalize(rows_in, norm_gain):
    values = rows_in.astype(jnp.float32)
    spread = jnp.mean(values * values, axis=-1, keepdims=True)
    return (values * lax.rsqrt(spread + norm_eps) * norm_gain).astype(jnp.bfloat16)


def attend(queries, keys_all, values_all, live_keys):
    scale_factor = 1.0 / math.sqrt(queries.shape[-1])
    scores = (
        jnp.einsum("qhe,khe->hqk", queries, keys_all, preferred_element_type=jnp.float32)
        * scale_factor
    )
    if live_keys is not None:
        scores = jnp.where(live_keys[None, None, :], scores, -1e30)
    row_max = jnp.max(scores, axis=-1, keepdims=True)
    weights = jnp.exp(scores - row_max)
    probabilities = (weights / jnp.sum(weights, axis=-1, keepdims=True)).astype(jnp.bfloat16)
    mixture = jnp.einsum(
        "hqk,khe->qhe", probabilities, values_all, preferred_element_type=jnp.float32
    )
    return mixture.reshape(mixture.shape[0], -1)


def shards_by_tile(
    tokens,
    cell_order,
    seam_rows,
    obs_mask,
    norm_gain,
    w_query,
    w_key,
    w_value,
    w_out,
    w_gate,
    w_up,
    w_down,
    w_read,
):
    round_count = lax.axis_size("round")
    model_count = lax.axis_size("mp")
    model_index = lax.axis_index("mp")
    round_index = lax.axis_index("round")
    width = tokens.shape[2]
    cell_dev = tokens.shape[1] // round_count
    permuted = tokens[:, cell_order, :]
    tile_tokens = lax.all_to_all(permuted, "round", split_axis=1, concat_axis=0, tiled=True)
    tile_rows = tile_tokens.shape[0] * cell_dev
    flat_tokens = tile_tokens.reshape(tile_rows, width)
    normed = normalize(flat_tokens, norm_gain)
    queries = jnp.dot(normed, w_query, preferred_element_type=jnp.float32).astype(jnp.bfloat16)
    keys_all = jnp.dot(normed, w_key, preferred_element_type=jnp.float32).astype(jnp.bfloat16)
    values_all = jnp.dot(normed, w_value, preferred_element_type=jnp.float32).astype(jnp.bfloat16)
    head_width = queries.shape[1]
    heads_dev = head_width // HDIM
    block_rows = min(512, tile_rows)
    query_blocks = queries.reshape(tile_rows // block_rows, block_rows, heads_dev, HDIM)
    key_heads = keys_all.reshape(tile_rows, heads_dev, HDIM)
    value_heads = values_all.reshape(tile_rows, heads_dev, HDIM)
    local_attn = lax.map(
        lambda query_block: attend(query_block, key_heads, value_heads, None), query_blocks
    )
    local_attn = local_attn.reshape(tile_rows, head_width)
    live_slot = seam_rows[0] >= 0
    safe_rows = jnp.where(live_slot, seam_rows[0], 0)
    packet = (
        lax.all_to_all(queries[safe_rows], "round", split_axis=0, concat_axis=0, tiled=True),
        lax.all_to_all(keys_all[safe_rows], "round", split_axis=0, concat_axis=0, tiled=True),
        lax.all_to_all(values_all[safe_rows], "round", split_axis=0, concat_axis=0, tiled=True),
        lax.all_to_all(
            live_slot.astype(jnp.bfloat16), "round", split_axis=0, concat_axis=0, tiled=True
        ),
    )
    seam_queries = packet[0].reshape(-1, heads_dev, HDIM)
    seam_keys = packet[1].reshape(-1, heads_dev, HDIM)
    seam_values = packet[2].reshape(-1, heads_dev, HDIM)
    seam_live = packet[3].reshape(-1) > 0.5
    seam_attn = attend(seam_queries, seam_keys, seam_values, seam_live).astype(jnp.bfloat16)
    returned = lax.all_to_all(
        seam_attn.reshape(round_count, -1, head_width),
        "round",
        split_axis=0,
        concat_axis=0,
        tiled=True,
    )
    target = jnp.where(live_slot, seam_rows[0], tile_rows).reshape(-1)
    combined = (
        local_attn.at[target]
        .add(returned.reshape(-1, head_width).astype(jnp.float32), mode="drop")
        .astype(jnp.bfloat16)
    )
    share_rows = tile_rows // model_count
    own_first = model_index * share_rows
    gate_part = jnp.dot(normed, w_gate, preferred_element_type=jnp.float32)
    up_part = jnp.dot(normed, w_up, preferred_element_type=jnp.float32)
    hidden = (jax.nn.silu(gate_part) * up_part).astype(jnp.bfloat16)
    attn_part = jnp.dot(combined, w_out, preferred_element_type=jnp.float32)
    summed = lax.psum_scatter(
        attn_part + jnp.dot(hidden, w_down, preferred_element_type=jnp.float32),
        "mp",
        scatter_dimension=0,
        tiled=True,
    )
    own_rows = lax.dynamic_slice_in_dim(flat_tokens, own_first, share_rows, 0)
    result_rows = (own_rows.astype(jnp.float32) + summed).astype(jnp.bfloat16)
    tiles_out = result_rows.reshape(share_rows // cell_dev, cell_dev, width)
    my_cells = lax.dynamic_slice_in_dim(cell_order, round_index * cell_dev, cell_dev)
    support = obs_mask[:, my_cells].astype(jnp.float32)
    partial_sum = jnp.einsum(
        "oc,rcd->od", support, tiles_out.astype(jnp.float32), precision=lax.Precision.HIGHEST
    )
    support_count = round_count * jnp.sum(obs_mask.astype(jnp.float32), axis=1)
    divisor = jnp.sqrt(support_count)
    pooled = lax.psum(partial_sum, ("round", "mp"))
    obs_logits = jnp.dot(pooled, w_read, precision=lax.Precision.HIGHEST) / divisor
    return (tiles_out, obs_logits)


def iota(shape, dimension):
    return lax.broadcasted_iota(jnp.int32, shape, dimension)


def one_hot(condition):
    return jnp.where(condition, 1.0, 0.0).astype(jnp.bfloat16)


def dot(left, right):
    return jnp.dot(left, right, preferred_element_type=jnp.float32)


def dot_t(left, right):
    return lax.dot_general(
        left, right, (((1,), (1,)), ((), ())), preferred_element_type=jnp.float32
    )


def split_three(values):
    high = values.astype(jnp.bfloat16)
    rest = values - high.astype(jnp.float32)
    middle = rest.astype(jnp.bfloat16)
    low = (rest - middle.astype(jnp.float32)).astype(jnp.bfloat16)
    return jnp.concatenate([high, middle, low], axis=0)


def attend_by_keys(head_vals, scores):
    weights = jnp.exp(scores - jnp.max(scores, axis=0, keepdims=True))
    probabilities = (weights / jnp.sum(weights, axis=0, keepdims=True)).astype(jnp.bfloat16)
    return dot(head_vals, probabilities)


def fetch_steps(rounds):
    return [((k, 0), (k, 1)) for k in range(rounds - 2, 0, -2)] + [((0, 1), (0, 1))]


def slot_steps(rounds):
    steps = [((0, 0), (0, 0))]
    for even, odd in fetch_steps(rounds):
        steps += [(even, odd)] if even == odd else [(even, odd), (odd, even)]
    return steps


def pack_kernel(tokens, seam_rows, block, landed, padded, arrivals):
    width = tokens.shape[2]
    slots, owners = seam_rows.shape[1:]
    copies = [
        pltpu.make_async_copy(seam_rows.at[0], landed, arrivals.at[0]),
        pltpu.make_async_copy(tokens, block.at[:, :, :width], arrivals.at[1]),
    ]
    for copy in copies:
        copy.start()
    padded[...] = jnp.zeros(padded.shape, jnp.float32)
    copies[0].wait()
    row = iota((tokens.shape[1], owners), 0)
    held = row == landed[:1]
    for slot in range(1, slots):
        held = held | (row == landed[slot : slot + 1])
    padded[:, :owners] = jnp.where(held, 1.0, 0.0)
    block[0, :, width:] = padded[...].astype(jnp.bfloat16)
    copies[1].wait()


def early_kernel(prepare, *refs):
    @pl.when(lax.axis_index("round") == 0)
    def _():
        prepare(*refs)


def late_kernel(prepare, given, made, *refs):
    @pl.when(lax.axis_index("round") != 0)
    def _():
        prepare(*refs[:given], *refs[given + made :])


def prepare(rounds, cells, counts, *refs):
    order_in, mask_in, *copied = refs[: counts + 2]
    rest = refs[counts + 2 :]
    w_read, w_down, w_out, gain, w_gate, w_up, w_query_key = rest[:7]
    w_value_t, read_down, read_out = rest[7:10]
    picks, token_picks, place, tile_bias, divisor = rest[10:15]
    order, mask, w_value, arrivals = rest[15:]
    half = w_query_key.shape[1] // 2
    w_query, w_key = w_query_key.at[:, :half], w_query_key.at[:, half:]
    targets = (order, mask, w_read, w_value, w_down, w_out, gain, w_query, w_key, w_gate, w_up)
    copies = [
        pltpu.make_async_copy(source, target, arrivals.at[k])
        for k, (source, target) in enumerate(zip((order_in, mask_in, *copied), targets))
    ]
    for copy in copies:
        copy.start()
    me, model = lax.axis_index("round"), lax.axis_index("mp")
    core = model & 1
    cell_dev = cells // rounds
    tile_rows = rounds * cell_dev
    share = tile_rows // 4
    total = rounds * cells
    observables = mask.shape[0]

    def slot_round(slot):
        shift, flip = jnp.zeros_like(slot), jnp.zeros_like(slot)
        for k, (even, odd) in enumerate(slot_steps(rounds)):
            shift = jnp.where(slot == k, jnp.where(core == 0, even[0], odd[0]), shift)
            flip = jnp.where(slot == k, jnp.where(core == 0, even[1], odd[1]), flip)
        return ((me + rounds - shift) & (rounds - 1)) ^ flip

    for copy in copies[:2]:
        copy.wait()
    row = iota((total, 1), 0)
    placed = order[...] == lax.rem(row, cells)
    along = iota((1, cells), 1)
    position = jnp.sum(jnp.where(placed, along, 0), axis=1, keepdims=True)
    tile = lax.div(position, cell_dev)
    in_tile = slot_round(lax.div(row, cells)) * cell_dev + lax.rem(position, cell_dev)
    column = iota((1, total), 1)
    slot_start = slot_round(lax.div(column, cells)) * tile_rows
    place[...] = one_hot(tile * tile_rows + in_tile == slot_start + lax.rem(column, cells))
    along_rows = jnp.broadcast_to(along.astype(jnp.float32), (8, cells)).astype(jnp.bfloat16)
    position_row = dot_t(along_rows, one_hot(placed))[:1].astype(jnp.int32)
    tile_row = lax.div(position_row, cell_dev)
    in_tile_row = slot_round(lax.div(column, cells)) * cell_dev + lax.rem(position_row, cell_dev)
    tile_bias[...] = jnp.where(tile == tile_row, 0.0, -1e30)

    index = iota((tile_rows, 1), 0)
    quarter = lax.div(index, share)
    target_model = jnp.where(quarter < 2, model ^ 1, model) ^ jnp.where((quarter & 1) == 0, 3, 0)
    target = target_model * share + lax.rem(index, share)
    own = one_hot((tile_row == me) & (in_tile_row == target))
    mask_bf = mask[...].astype(jnp.float32).astype(jnp.bfloat16)
    support = dot(mask_bf, one_hot(iota((cells, 1), 0) == lax.rem(column, cells))).astype(
        jnp.bfloat16
    )
    picks[:tile_rows] = own
    picks[tile_rows:] = support
    token_picks[:tile_rows] = jnp.where(quarter == 3, own, jnp.zeros_like(own))
    token_picks[tile_rows:] = jnp.where(model == 0, support, jnp.zeros_like(support))
    count = rounds * jnp.sum(mask[...].astype(jnp.float32), axis=1, keepdims=True)
    divisor[...] = jnp.broadcast_to(jnp.sqrt(count), divisor.shape)

    for copy in copies[2:6]:
        copy.wait()
    head_width = w_value.shape[1]
    identity = one_hot(iota((head_width, 1), 0) == iota((1, head_width), 1))
    w_value_t[...] = dot_t(identity, w_value[...]).astype(jnp.bfloat16)
    read_parts = split_three(jnp.broadcast_to(w_read[...], (8, w_read.shape[1])))
    for weight, read in ((w_down, read_down), (w_out, read_out)):
        parts = dot_t(read_parts, weight[...])
        read[...] = parts[:1] + parts[8:9] + parts[16:17]
    for copy in copies[6:]:
        copy.wait()


def layer_kernel(cells, slots, *refs):
    blocks, rest = refs[:slots], refs[slots:]
    w_read, w_down, w_out, gain, w_gate, w_up, w_query_key = rest[:7]
    w_value_t, read_down, read_out = rest[7:10]
    picks, token_picks, place, tile_bias, divisor = rest[10:15]
    outs = rest[15:]
    total = slots * cells
    width = gain.shape[1]
    head_width = w_query_key.shape[1] // 2
    observables = divisor.shape[0]
    tile_rows = picks.shape[0] - observables

    tokens = jnp.concatenate([block[0, :, :width] for block in blocks], axis=0)
    token_rows = dot(token_picks[...], tokens)

    members = jnp.concatenate([block[0, :, width:] for block in blocks], axis=0)
    member = dot(place[...], members).astype(jnp.bfloat16)

    values = tokens.astype(jnp.float32)
    spread = jnp.mean(values * values, axis=-1, keepdims=True)
    normed = (values * lax.rsqrt(spread + norm_eps) * gain[...]).astype(jnp.bfloat16)

    vals = dot_t(w_value_t[...], normed).astype(jnp.bfloat16)
    query_key = dot(normed, w_query_key[...])
    keys = query_key[:, head_width:].astype(jnp.bfloat16)
    queries = (query_key[:, :head_width] * (1.0 / math.sqrt(HDIM))).astype(jnp.bfloat16)

    gate = dot(normed, w_gate[...])
    up = dot(normed, w_up[...])
    hidden = (gate / (1.0 + jnp.exp(-gate)) * up).astype(jnp.bfloat16)

    seam_bias = jnp.where(dot_t(member, member) > 0.5, 0.0, -1e30)
    in_seam = dot_t(jnp.ones((8, LANES), jnp.bfloat16), member)[:1] > 0.5
    lane_head = lax.div(iota((1, head_width), 1), HDIM)
    parts = []
    for first in range(0, total, LANES):
        some = slice(first, first + LANES)
        mixed = []
        for head in range(head_width // HDIM):
            head_keys = jnp.where(lane_head == head, keys, jnp.zeros_like(keys))
            head_vals = vals[head * HDIM : (head + 1) * HDIM]
            scores = dot_t(head_keys, queries[some])
            local = attend_by_keys(head_vals, scores + tile_bias[:, some])
            seam = attend_by_keys(head_vals, scores + seam_bias[:, some])
            seam = seam.astype(jnp.bfloat16).astype(jnp.float32)
            mixed.append((local + jnp.where(in_seam[:, some], seam, 0.0)).astype(jnp.bfloat16))
        parts.append(jnp.concatenate(mixed, axis=0))
    combined = jnp.concatenate(parts, axis=1)

    hidden_rows = dot(picks[...], hidden)
    combined_rows = dot_t(picks[...], combined)
    update = (
        token_rows[:tile_rows]
        + dot(hidden_rows[:tile_rows].astype(jnp.bfloat16), w_down[...])
        + dot(combined_rows[:tile_rows].astype(jnp.bfloat16), w_out[...])
    )
    logits = sum(
        jnp.sum(sums[tile_rows:] * read[...], axis=1, keepdims=True)
        for sums, read in (
            (hidden_rows, read_down),
            (combined_rows, read_out),
            (token_rows, w_read),
        )
    )
    logits = logits / divisor[:, :1]
    diagonal = iota((observables, LANES), 0) == iota((observables, LANES), 1)
    logits_row = jnp.sum(jnp.where(diagonal, logits, 0.0), axis=0, keepdims=True)
    share = tile_rows // 4
    send_over, send_stay, keep_over, keep_stay = outs
    for k, (over, stay) in enumerate(((send_over, send_stay), (keep_over, keep_stay))):
        over[:, :width] = update[2 * k * share : (2 * k + 1) * share]
        over[:, width:] = jnp.broadcast_to(logits_row, (share, LANES))
        stay[...] = update[(2 * k + 1) * share : (2 * k + 2) * share]


def finish_kernel(over, arrived, stay, other_stay, tiles_out, logits_out):
    count, cell_dev = tiles_out.shape[:2]
    width = stay.shape[1]
    rows = stay[...] + other_stay[...] + arrived[:, :width]
    for k in range(count):
        tiles_out[k] = rows[k * cell_dev : (k + 1) * cell_dev].astype(tiles_out.dtype)
    logits = over[:1, width:] + arrived[:1, width:]
    logits_out[...] = logits[:, : logits_out.shape[1]]


def shards_whole(
    tokens,
    cell_order,
    seam_rows,
    obs_mask,
    norm_gain,
    w_query,
    w_key,
    w_value,
    w_out,
    w_gate,
    w_up,
    w_down,
    w_read,
):
    rounds = lax.axis_size("round")
    models = lax.axis_size("mp")
    cells, width = tokens.shape[1:]
    cell_dev = cells // rounds
    tile_rows = rounds * cell_dev
    share = tile_rows // models
    total = rounds * cells
    observables = obs_mask.shape[0]
    vmem = pl.BlockSpec(memory_space=pltpu.VMEM)
    hbm = pl.BlockSpec(memory_space=pltpu.HBM)

    def pin(arrays, space):
        return [pltpu.with_memory_space_constraint(array, space) for array in arrays]

    brought = [
        w_read.reshape(1, -1),
        w_value,
        w_down,
        w_out,
        norm_gain.reshape(1, -1),
        w_query,
        w_key,
        w_gate,
        w_up,
    ]
    sources = pin([cell_order.reshape(1, -1), obs_mask, *brought], pltpu.HBM)
    made = [pltpu.VMEM(array.shape, array.dtype) for array in brought if not any(array is w for w in (w_value, w_query, w_key))] + [
        pltpu.VMEM((width, 2 * w_query.shape[1]), w_query.dtype),
        pltpu.VMEM(w_value.shape[::-1], w_value.dtype),
        pltpu.VMEM((1, w_down.shape[0]), jnp.float32),
        pltpu.VMEM((1, w_out.shape[0]), jnp.float32),
        pltpu.VMEM((tile_rows + observables, total), jnp.bfloat16),
        pltpu.VMEM((tile_rows + observables, total), jnp.bfloat16),
        pltpu.VMEM((total, total), jnp.bfloat16),
        pltpu.VMEM((total, total), jnp.float32),
        pltpu.VMEM((observables, LANES), jnp.float32),
    ]
    scratch = [
        pltpu.VMEM((1, cells), jnp.int32),
        pltpu.VMEM(obs_mask.shape, jnp.int32),
        pltpu.VMEM(w_value.shape, w_value.dtype),
        pltpu.SemaphoreType.DMA((len(sources),)),
    ]
    small = pltpu.CompilerParams(vmem_limit_bytes=SMALL_LIMIT)
    preparation = functools.partial(prepare, rounds, cells, len(brought))
    block = pl.pallas_call(
        pack_kernel,
        out_shape=pltpu.VMEM((1, cells, width + LANES), jnp.bfloat16),
        in_specs=[hbm, hbm],
        out_specs=vmem,
        scratch_shapes=[
            pltpu.VMEM(seam_rows.shape[:0:-1], jnp.int32),
            pltpu.VMEM((cells, LANES), jnp.float32),
            pltpu.SemaphoreType.DMA((2,)),
        ],
        compiler_params=small,
    )(*pin([tokens, seam_rows.transpose(0, 2, 1)], pltpu.HBM))
    prepared = pl.pallas_call(
        functools.partial(early_kernel, preparation),
        out_shape=made,
        in_specs=[hbm] * len(sources),
        out_specs=[vmem] * len(made),
        scratch_shapes=scratch,
        compiler_params=small,
    )(*sources)
    block, prepared = lax.optimization_barrier((block, prepared))

    def fetch(even, odd):
        across = 1 if even == odd else 0
        pairs = []
        for r in range(rounds):
            for m in range(models):
                shift, flip = odd if m & 1 else even
                source = ((r - shift) % rounds) ^ flip
                pairs.append((source * models + (m ^ across), r * models + m))
        return lax.ppermute(block, ("round", "mp"), pairs)

    def other_core(array):
        return lax.ppermute(array, "mp", [(m, m ^ 1) for m in range(models)])

    direct = [fetch(even, odd) for even, odd in fetch_steps(rounds)]
    prepared = pl.pallas_call(
        functools.partial(late_kernel, preparation, len(sources), len(made)),
        out_shape=made,
        in_specs=[hbm] * len(sources) + [vmem] * len(made),
        out_specs=[vmem] * len(made),
        input_output_aliases={len(sources) + k: k for k in range(len(made))},
        scratch_shapes=scratch,
        compiler_params=small,
        cost_estimate=pl.CostEstimate(flops=0, bytes_accessed=8 * 1024 * 1024, transcendentals=0),
    )(*sources, *pin(prepared, pltpu.VMEM))

    direct[-2], prepared = lax.optimization_barrier((direct[-2], prepared))
    blocks = [block]
    for (even, odd), fetched in zip(fetch_steps(rounds), direct):
        blocks += [fetched] if even == odd else [fetched, other_core(fetched)]

    over = pltpu.VMEM((share, width + LANES), jnp.float32)
    stay = pltpu.VMEM((share, width), jnp.float32)
    send_over, send_stay, keep_over, keep_stay = pl.pallas_call(
        functools.partial(layer_kernel, cells, len(blocks)),
        out_shape=(over, stay, over, stay),
        in_specs=[vmem] * (len(blocks) + len(prepared)),
        out_specs=(vmem,) * 4,
        compiler_params=pltpu.CompilerParams(vmem_limit_bytes=LAYER_LIMIT),
    )(*pin([*blocks, *prepared], pltpu.VMEM))
    over = keep_over + other_core(send_over)
    arrived = lax.ppermute(over, "mp", [(m, m ^ 3) for m in range(models)])
    other_stay = other_core(send_stay)
    tiles_out, logits = pl.pallas_call(
        finish_kernel,
        out_shape=(
            jax.ShapeDtypeStruct((share // cell_dev, cell_dev, width), jnp.bfloat16),
            jax.ShapeDtypeStruct((1, observables), jnp.float32),
        ),
        in_specs=[vmem] * 4,
        out_specs=(vmem, vmem),
        compiler_params=pltpu.CompilerParams(vmem_limit_bytes=SMALL_LIMIT),
    )(*pin([over, arrived, keep_stay, other_stay], pltpu.VMEM))
    return tiles_out, logits.reshape(-1)


def fits_whole(mesh, tokens, seam_rows, w_query):
    rounds, models = mesh.shape["round"], mesh.shape["mp"]
    total = tokens.shape[0] * tokens.shape[1]
    share = total // rounds // models
    return (
        models == 4
        and rounds == tokens.shape[0]
        and rounds & (rounds - 1) == 0
        and rounds > 2
        and total <= 512
        and total % LANES == 0
        and total // rounds <= 256
        and share % 8 == 0
        and tokens.shape[1] % 16 == 0
        and seam_rows.shape[2] == 2
        and w_query.shape[1] // models % HDIM == 0
    )


def solution(mesh):
    def layer(*args):
        tokens, seam_rows, w_query = args[0], args[2], args[5]
        whole = fits_whole(mesh, tokens, seam_rows, w_query)
        return placed(mesh, shards_whole if whole else shards_by_tile)(*args)

    return layer


def placed(mesh, shards):
    return jax.shard_map(
        shards,
        mesh=mesh,
        in_specs=(
            P("round", None, None),
            P(),
            P("round", None, None),
            P(),
            P(),
            P(None, "mp"),
            P(None, "mp"),
            P(None, "mp"),
            P("mp", None),
            P(None, "mp"),
            P(None, "mp"),
            P("mp", None),
            P(),
        ),
        out_specs=(P("mp", "round", None), P()),
        check_vma=False,
    )
```

```python
import functools
import math

import jax
import jax.numpy as jnp
from jax import lax
from jax.experimental import pallas as pl
from jax.experimental.pallas import tpu as pltpu
from jax.sharding import PartitionSpec as P

HDIM = 64
LANES = 128
SMALL_LIMIT = 8 * 1024 * 1024
LAYER_LIMIT = 32 * 1024 * 1024


norm_eps = 1e-06


def normalize(rows_in, norm_gain):
    values = rows_in.astype(jnp.float32)
    spread = jnp.mean(values * values, axis=-1, keepdims=True)
    return (values * lax.rsqrt(spread + norm_eps) * norm_gain).astype(jnp.bfloat16)


def attend(queries, keys_all, values_all, live_keys):
    scale_factor = 1.0 / math.sqrt(queries.shape[-1])
    scores = (
        jnp.einsum("qhe,khe->hqk", queries, keys_all, preferred_element_type=jnp.float32)
        * scale_factor
    )
    if live_keys is not None:
        scores = jnp.where(live_keys[None, None, :], scores, -1e30)
    row_max = jnp.max(scores, axis=-1, keepdims=True)
    weights = jnp.exp(scores - row_max)
    probabilities = (weights / jnp.sum(weights, axis=-1, keepdims=True)).astype(jnp.bfloat16)
    mixture = jnp.einsum(
        "hqk,khe->qhe", probabilities, values_all, preferred_element_type=jnp.float32
    )
    return mixture.reshape(mixture.shape[0], -1)


def shards_by_tile(
    tokens,
    cell_order,
    seam_rows,
    obs_mask,
    norm_gain,
    w_query,
    w_key,
    w_value,
    w_out,
    w_gate,
    w_up,
    w_down,
    w_read,
):
    round_count = lax.axis_size("round")
    model_count = lax.axis_size("mp")
    model_index = lax.axis_index("mp")
    round_index = lax.axis_index("round")
    width = tokens.shape[2]
    cell_dev = tokens.shape[1] // round_count
    permuted = tokens[:, cell_order, :]
    tile_tokens = lax.all_to_all(permuted, "round", split_axis=1, concat_axis=0, tiled=True)
    tile_rows = tile_tokens.shape[0] * cell_dev
    flat_tokens = tile_tokens.reshape(tile_rows, width)
    normed = normalize(flat_tokens, norm_gain)
    queries = jnp.dot(normed, w_query, preferred_element_type=jnp.float32).astype(jnp.bfloat16)
    keys_all = jnp.dot(normed, w_key, preferred_element_type=jnp.float32).astype(jnp.bfloat16)
    values_all = jnp.dot(normed, w_value, preferred_element_type=jnp.float32).astype(jnp.bfloat16)
    head_width = queries.shape[1]
    heads_dev = head_width // HDIM
    block_rows = min(512, tile_rows)
    query_blocks = queries.reshape(tile_rows // block_rows, block_rows, heads_dev, HDIM)
    key_heads = keys_all.reshape(tile_rows, heads_dev, HDIM)
    value_heads = values_all.reshape(tile_rows, heads_dev, HDIM)
    local_attn = lax.map(
        lambda query_block: attend(query_block, key_heads, value_heads, None), query_blocks
    )
    local_attn = local_attn.reshape(tile_rows, head_width)
    live_slot = seam_rows[0] >= 0
    safe_rows = jnp.where(live_slot, seam_rows[0], 0)
    packet = (
        lax.all_to_all(queries[safe_rows], "round", split_axis=0, concat_axis=0, tiled=True),
        lax.all_to_all(keys_all[safe_rows], "round", split_axis=0, concat_axis=0, tiled=True),
        lax.all_to_all(values_all[safe_rows], "round", split_axis=0, concat_axis=0, tiled=True),
        lax.all_to_all(
            live_slot.astype(jnp.bfloat16), "round", split_axis=0, concat_axis=0, tiled=True
        ),
    )
    seam_queries = packet[0].reshape(-1, heads_dev, HDIM)
    seam_keys = packet[1].reshape(-1, heads_dev, HDIM)
    seam_values = packet[2].reshape(-1, heads_dev, HDIM)
    seam_live = packet[3].reshape(-1) > 0.5
    seam_attn = attend(seam_queries, seam_keys, seam_values, seam_live).astype(jnp.bfloat16)
    returned = lax.all_to_all(
        seam_attn.reshape(round_count, -1, head_width),
        "round",
        split_axis=0,
        concat_axis=0,
        tiled=True,
    )
    target = jnp.where(live_slot, seam_rows[0], tile_rows).reshape(-1)
    combined = (
        local_attn.at[target]
        .add(returned.reshape(-1, head_width).astype(jnp.float32), mode="drop")
        .astype(jnp.bfloat16)
    )
    share_rows = tile_rows // model_count
    own_first = model_index * share_rows
    gate_part = jnp.dot(normed, w_gate, preferred_element_type=jnp.float32)
    up_part = jnp.dot(normed, w_up, preferred_element_type=jnp.float32)
    hidden = (jax.nn.silu(gate_part) * up_part).astype(jnp.bfloat16)
    attn_part = jnp.dot(combined, w_out, preferred_element_type=jnp.float32)
    summed = lax.psum_scatter(
        attn_part + jnp.dot(hidden, w_down, preferred_element_type=jnp.float32),
        "mp",
        scatter_dimension=0,
        tiled=True,
    )
    own_rows = lax.dynamic_slice_in_dim(flat_tokens, own_first, share_rows, 0)
    result_rows = (own_rows.astype(jnp.float32) + summed).astype(jnp.bfloat16)
    tiles_out = result_rows.reshape(share_rows // cell_dev, cell_dev, width)
    my_cells = lax.dynamic_slice_in_dim(cell_order, round_index * cell_dev, cell_dev)
    support = obs_mask[:, my_cells].astype(jnp.float32)
    partial_sum = jnp.einsum(
        "oc,rcd->od", support, tiles_out.astype(jnp.float32), precision=lax.Precision.HIGHEST
    )
    support_count = round_count * jnp.sum(obs_mask.astype(jnp.float32), axis=1)
    divisor = jnp.sqrt(support_count)
    pooled = lax.psum(partial_sum, ("round", "mp"))
    obs_logits = jnp.dot(pooled, w_read, precision=lax.Precision.HIGHEST) / divisor
    return (tiles_out, obs_logits)


def iota(shape, dimension):
    return lax.broadcasted_iota(jnp.int32, shape, dimension)


def one_hot(condition):
    return jnp.where(condition, 1.0, 0.0).astype(jnp.bfloat16)


def dot(left, right):
    return jnp.dot(left, right, preferred_element_type=jnp.float32)


def dot_t(left, right):
    return lax.dot_general(
        left, right, (((1,), (1,)), ((), ())), preferred_element_type=jnp.float32
    )


def split_three(values):
    high = values.astype(jnp.bfloat16)
    rest = values - high.astype(jnp.float32)
    middle = rest.astype(jnp.bfloat16)
    low = (rest - middle.astype(jnp.float32)).astype(jnp.bfloat16)
    return jnp.concatenate([high, middle, low], axis=0)


def attend_by_keys(head_vals, scores):
    weights = jnp.exp(scores - jnp.max(scores, axis=0, keepdims=True))
    probabilities = (weights / jnp.sum(weights, axis=0, keepdims=True)).astype(jnp.bfloat16)
    return dot(head_vals, probabilities)


def fetch_steps(rounds):
    return [((k, 0), (k, 1)) for k in range(rounds - 2, 0, -2)] + [((0, 1), (0, 1))]


def slot_steps(rounds):
    steps = [((0, 0), (0, 0))]
    for even, odd in fetch_steps(rounds):
        steps += [(even, odd)] if even == odd else [(even, odd), (odd, even)]
    return steps


def pack_kernel(tokens, seam_rows, block, landed, padded, arrivals):
    width = tokens.shape[2]
    slots, owners = seam_rows.shape[1:]
    copies = [
        pltpu.make_async_copy(seam_rows.at[0], landed, arrivals.at[0]),
        pltpu.make_async_copy(tokens, block.at[:, :, :width], arrivals.at[1]),
    ]
    for copy in copies:
        copy.start()
    padded[...] = jnp.zeros(padded.shape, jnp.float32)
    copies[0].wait()
    row = iota((tokens.shape[1], owners), 0)
    held = row == landed[:1]
    for slot in range(1, slots):
        held = held | (row == landed[slot : slot + 1])
    padded[:, :owners] = jnp.where(held, 1.0, 0.0)
    block[0, :, width:] = padded[...].astype(jnp.bfloat16)
    copies[1].wait()


def early_kernel(prepare, *refs):
    @pl.when(lax.axis_index("round") == 0)
    def _():
        prepare(*refs)


def late_kernel(prepare, given, made, *refs):
    @pl.when(lax.axis_index("round") != 0)
    def _():
        prepare(*refs[:given], *refs[given + made :])


def prepare(rounds, cells, counts, *refs):
    order_in, mask_in, *copied = refs[: counts + 2]
    rest = refs[counts + 2 :]
    w_read, w_down, w_out, gain, w_query, w_key, w_gate, w_up = rest[:8]
    w_value_t, read_down, read_out = rest[8:11]
    picks, token_picks, place, tile_bias, divisor = rest[11:16]
    order, mask, w_value, arrivals = rest[16:]
    targets = (order, mask, w_read, w_value, w_down, w_out, gain, w_query, w_key, w_gate, w_up)
    copies = [
        pltpu.make_async_copy(source, target, arrivals.at[k])
        for k, (source, target) in enumerate(zip((order_in, mask_in, *copied), targets))
    ]
    for copy in copies:
        copy.start()
    me, model = lax.axis_index("round"), lax.axis_index("mp")
    core = model & 1
    cell_dev = cells // rounds
    tile_rows = rounds * cell_dev
    share = tile_rows // 4
    total = rounds * cells
    observables = mask.shape[0]

    def slot_round(slot):
        shift, flip = jnp.zeros_like(slot), jnp.zeros_like(slot)
        for k, (even, odd) in enumerate(slot_steps(rounds)):
            shift = jnp.where(slot == k, jnp.where(core == 0, even[0], odd[0]), shift)
            flip = jnp.where(slot == k, jnp.where(core == 0, even[1], odd[1]), flip)
        return ((me + rounds - shift) & (rounds - 1)) ^ flip

    for copy in copies[:2]:
        copy.wait()
    row = iota((total, 1), 0)
    placed = order[...] == lax.rem(row, cells)
    along = iota((1, cells), 1)
    position = jnp.sum(jnp.where(placed, along, 0), axis=1, keepdims=True)
    tile = lax.div(position, cell_dev)
    in_tile = slot_round(lax.div(row, cells)) * cell_dev + lax.rem(position, cell_dev)
    column = iota((1, total), 1)
    slot_start = slot_round(lax.div(column, cells)) * tile_rows
    place[...] = one_hot(tile * tile_rows + in_tile == slot_start + lax.rem(column, cells))
    along_rows = jnp.broadcast_to(along.astype(jnp.float32), (8, cells)).astype(jnp.bfloat16)
    position_row = dot_t(along_rows, one_hot(placed))[:1].astype(jnp.int32)
    tile_row = lax.div(position_row, cell_dev)
    in_tile_row = slot_round(lax.div(column, cells)) * cell_dev + lax.rem(position_row, cell_dev)
    tile_bias[...] = jnp.where(tile == tile_row, 0.0, -1e30)

    index = iota((tile_rows, 1), 0)
    quarter = lax.div(index, share)
    target_model = jnp.where(quarter < 2, model ^ 1, model) ^ jnp.where((quarter & 1) == 0, 3, 0)
    target = target_model * share + lax.rem(index, share)
    own = one_hot((tile_row == me) & (in_tile_row == target))
    mask_bf = mask[...].astype(jnp.float32).astype(jnp.bfloat16)
    support = dot(mask_bf, one_hot(iota((cells, 1), 0) == lax.rem(column, cells))).astype(
        jnp.bfloat16
    )
    picks[:tile_rows] = own
    picks[tile_rows:] = support
    token_picks[:tile_rows] = jnp.where(quarter == 3, own, jnp.zeros_like(own))
    token_picks[tile_rows:] = jnp.where(model == 0, support, jnp.zeros_like(support))
    count = rounds * jnp.sum(mask[...].astype(jnp.float32), axis=1, keepdims=True)
    divisor[...] = jnp.broadcast_to(jnp.sqrt(count), divisor.shape)

    for copy in copies[2:6]:
        copy.wait()
    head_width = w_value.shape[1]
    identity = one_hot(iota((head_width, 1), 0) == iota((1, head_width), 1))
    w_value_t[...] = dot_t(identity, w_value[...]).astype(jnp.bfloat16)
    read_parts = split_three(jnp.broadcast_to(w_read[...], (8, w_read.shape[1])))
    for weight, read in ((w_down, read_down), (w_out, read_out)):
        parts = dot_t(read_parts, weight[...])
        read[...] = parts[:1] + parts[8:9] + parts[16:17]
    for copy in copies[6:]:
        copy.wait()


def layer_kernel(cells, slots, *refs):
    blocks, rest = refs[:slots], refs[slots:]
    w_read, w_down, w_out, gain, w_query, w_key, w_gate, w_up = rest[:8]
    w_value_t, read_down, read_out = rest[8:11]
    picks, token_picks, place, tile_bias, divisor = rest[11:16]
    outs = rest[16:]
    total = slots * cells
    width = gain.shape[1]
    head_width = w_query.shape[1]
    observables = divisor.shape[0]
    tile_rows = picks.shape[0] - observables

    tokens = jnp.concatenate([block[0, :, :width] for block in blocks], axis=0)
    token_rows = dot(token_picks[...], tokens)

    members = jnp.concatenate([block[0, :, width:] for block in blocks], axis=0)
    member = dot(place[...], members).astype(jnp.bfloat16)

    values = tokens.astype(jnp.float32)
    spread = jnp.mean(values * values, axis=-1, keepdims=True)
    normed = (values * lax.rsqrt(spread + norm_eps) * gain[...]).astype(jnp.bfloat16)

    vals = dot_t(w_value_t[...], normed).astype(jnp.bfloat16)
    queries = (dot(normed, w_query[...]) * (1.0 / math.sqrt(HDIM))).astype(jnp.bfloat16)
    keys = dot(normed, w_key[...]).astype(jnp.bfloat16)

    gate = dot(normed, w_gate[...])
    up = dot(normed, w_up[...])
    hidden = (gate / (1.0 + jnp.exp(-gate)) * up).astype(jnp.bfloat16)

    seam_bias = jnp.where(dot_t(member, member) > 0.5, 0.0, -1e30)
    in_seam = dot_t(jnp.ones((8, LANES), jnp.bfloat16), member)[:1] > 0.5
    lane_head = lax.div(iota((1, head_width), 1), HDIM)
    parts = []
    for first in range(0, total, LANES):
        some = slice(first, first + LANES)
        mixed = []
        for head in range(head_width // HDIM):
            head_keys = jnp.where(lane_head == head, keys, jnp.zeros_like(keys))
            head_vals = vals[head * HDIM : (head + 1) * HDIM]
            scores = dot_t(head_keys, queries[some])
            local = attend_by_keys(head_vals, scores + tile_bias[:, some])
            seam = attend_by_keys(head_vals, scores + seam_bias[:, some])
            seam = seam.astype(jnp.bfloat16).astype(jnp.float32)
            mixed.append((local + jnp.where(in_seam[:, some], seam, 0.0)).astype(jnp.bfloat16))
        parts.append(jnp.concatenate(mixed, axis=0))
    combined = jnp.concatenate(parts, axis=1)

    hidden_rows = dot(picks[...], hidden)
    combined_rows = dot_t(picks[...], combined)
    update = (
        token_rows[:tile_rows]
        + dot(hidden_rows[:tile_rows].astype(jnp.bfloat16), w_down[...])
        + dot(combined_rows[:tile_rows].astype(jnp.bfloat16), w_out[...])
    )
    logits = sum(
        jnp.sum(sums[tile_rows:] * read[...], axis=1, keepdims=True)
        for sums, read in (
            (hidden_rows, read_down),
            (combined_rows, read_out),
            (token_rows, w_read),
        )
    )
    logits = logits / divisor[:, :1]
    diagonal = iota((observables, LANES), 0) == iota((observables, LANES), 1)
    logits_row = jnp.sum(jnp.where(diagonal, logits, 0.0), axis=0, keepdims=True)
    share = tile_rows // 4
    send_over, send_stay, keep_over, keep_stay = outs
    for k, (over, stay) in enumerate(((send_over, send_stay), (keep_over, keep_stay))):
        over[:, :width] = update[2 * k * share : (2 * k + 1) * share]
        over[:, width:] = jnp.broadcast_to(logits_row, (share, LANES))
        stay[...] = update[(2 * k + 1) * share : (2 * k + 2) * share]


def finish_kernel(over, arrived, stay, other_stay, tiles_out, logits_out):
    count, cell_dev = tiles_out.shape[:2]
    width = stay.shape[1]
    rows = stay[...] + other_stay[...] + arrived[:, :width]
    for k in range(count):
        tiles_out[k] = rows[k * cell_dev : (k + 1) * cell_dev].astype(tiles_out.dtype)
    logits = over[:1, width:] + arrived[:1, width:]
    logits_out[...] = logits[:, : logits_out.shape[1]]


def shards_whole(
    tokens,
    cell_order,
    seam_rows,
    obs_mask,
    norm_gain,
    w_query,
    w_key,
    w_value,
    w_out,
    w_gate,
    w_up,
    w_down,
    w_read,
):
    rounds = lax.axis_size("round")
    models = lax.axis_size("mp")
    cells, width = tokens.shape[1:]
    cell_dev = cells // rounds
    tile_rows = rounds * cell_dev
    share = tile_rows // models
    total = rounds * cells
    observables = obs_mask.shape[0]
    vmem = pl.BlockSpec(memory_space=pltpu.VMEM)
    hbm = pl.BlockSpec(memory_space=pltpu.HBM)

    def pin(arrays, space):
        return [pltpu.with_memory_space_constraint(array, space) for array in arrays]

    brought = [
        w_read.reshape(1, -1),
        w_value,
        w_down,
        w_out,
        norm_gain.reshape(1, -1),
        w_query,
        w_key,
        w_gate,
        w_up,
    ]
    sources = pin([cell_order.reshape(1, -1), obs_mask, *brought], pltpu.HBM)
    made = [pltpu.VMEM(array.shape, array.dtype) for array in brought if array is not w_value] + [
        pltpu.VMEM(w_value.shape[::-1], w_value.dtype),
        pltpu.VMEM((1, w_down.shape[0]), jnp.float32),
        pltpu.VMEM((1, w_out.shape[0]), jnp.float32),
        pltpu.VMEM((tile_rows + observables, total), jnp.bfloat16),
        pltpu.VMEM((tile_rows + observables, total), jnp.bfloat16),
        pltpu.VMEM((total, total), jnp.bfloat16),
        pltpu.VMEM((total, total), jnp.float32),
        pltpu.VMEM((observables, LANES), jnp.float32),
    ]
    scratch = [
        pltpu.VMEM((1, cells), jnp.int32),
        pltpu.VMEM(obs_mask.shape, jnp.int32),
        pltpu.VMEM(w_value.shape, w_value.dtype),
        pltpu.SemaphoreType.DMA((len(sources),)),
    ]
    small = pltpu.CompilerParams(vmem_limit_bytes=SMALL_LIMIT)
    preparation = functools.partial(prepare, rounds, cells, len(brought))
    block = pl.pallas_call(
        pack_kernel,
        out_shape=pltpu.VMEM((1, cells, width + LANES), jnp.bfloat16),
        in_specs=[hbm, hbm],
        out_specs=vmem,
        scratch_shapes=[
            pltpu.VMEM(seam_rows.shape[:0:-1], jnp.int32),
            pltpu.VMEM((cells, LANES), jnp.float32),
            pltpu.SemaphoreType.DMA((2,)),
        ],
        compiler_params=small,
    )(*pin([tokens, seam_rows.transpose(0, 2, 1)], pltpu.HBM))
    prepared = pl.pallas_call(
        functools.partial(early_kernel, preparation),
        out_shape=made,
        in_specs=[hbm] * len(sources),
        out_specs=[vmem] * len(made),
        scratch_shapes=scratch,
        compiler_params=small,
    )(*sources)
    block, prepared = lax.optimization_barrier((block, prepared))

    def fetch(even, odd):
        across = 1 if even == odd else 0
        pairs = []
        for r in range(rounds):
            for m in range(models):
                shift, flip = odd if m & 1 else even
                source = ((r - shift) % rounds) ^ flip
                pairs.append((source * models + (m ^ across), r * models + m))
        return lax.ppermute(block, ("round", "mp"), pairs)

    def other_core(array):
        return lax.ppermute(array, "mp", [(m, m ^ 1) for m in range(models)])

    direct = [fetch(even, odd) for even, odd in fetch_steps(rounds)]
    prepared = pl.pallas_call(
        functools.partial(late_kernel, preparation, len(sources), len(made)),
        out_shape=made,
        in_specs=[hbm] * len(sources) + [vmem] * len(made),
        out_specs=[vmem] * len(made),
        input_output_aliases={len(sources) + k: k for k in range(len(made))},
        scratch_shapes=scratch,
        compiler_params=small,
        cost_estimate=pl.CostEstimate(flops=0, bytes_accessed=8 * 1024 * 1024, transcendentals=0),
    )(*sources, *pin(prepared, pltpu.VMEM))

    direct[-2], prepared = lax.optimization_barrier((direct[-2], prepared))
    blocks = [block]
    for (even, odd), fetched in zip(fetch_steps(rounds), direct):
        blocks += [fetched] if even == odd else [fetched, other_core(fetched)]

    over = pltpu.VMEM((share, width + LANES), jnp.float32)
    stay = pltpu.VMEM((share, width), jnp.float32)
    send_over, send_stay, keep_over, keep_stay = pl.pallas_call(
        functools.partial(layer_kernel, cells, len(blocks)),
        out_shape=(over, stay, over, stay),
        in_specs=[vmem] * (len(blocks) + len(prepared)),
        out_specs=(vmem,) * 4,
        compiler_params=pltpu.CompilerParams(vmem_limit_bytes=LAYER_LIMIT),
    )(*pin([*blocks, *prepared], pltpu.VMEM))
    over = keep_over + other_core(send_over)
    arrived = lax.ppermute(over, "mp", [(m, m ^ 3) for m in range(models)])
    other_stay = other_core(send_stay)
    tiles_out, logits = pl.pallas_call(
        finish_kernel,
        out_shape=(
            jax.ShapeDtypeStruct((share // cell_dev, cell_dev, width), jnp.bfloat16),
            jax.ShapeDtypeStruct((1, observables), jnp.float32),
        ),
        in_specs=[vmem] * 4,
        out_specs=(vmem, vmem),
        compiler_params=pltpu.CompilerParams(vmem_limit_bytes=SMALL_LIMIT),
    )(*pin([over, arrived, keep_stay, other_stay], pltpu.VMEM))
    return tiles_out, logits.reshape(-1)


def fits_whole(mesh, tokens, seam_rows, w_query):
    rounds, models = mesh.shape["round"], mesh.shape["mp"]
    total = tokens.shape[0] * tokens.shape[1]
    share = total // rounds // models
    return (
        models == 4
        and rounds == tokens.shape[0]
        and rounds & (rounds - 1) == 0
        and rounds > 2
        and total <= 512
        and total % LANES == 0
        and total // rounds <= 256
        and share % 8 == 0
        and tokens.shape[1] % 16 == 0
        and seam_rows.shape[2] == 2
        and w_query.shape[1] // models % HDIM == 0
    )


def solution(mesh):
    def layer(*args):
        tokens, seam_rows, w_query = args[0], args[2], args[5]
        whole = fits_whole(mesh, tokens, seam_rows, w_query)
        return placed(mesh, shards_whole if whole else shards_by_tile)(*args)

    return layer


def placed(mesh, shards):
    return jax.shard_map(
        shards,
        mesh=mesh,
        in_specs=(
            P("round", None, None),
            P(),
            P("round", None, None),
            P(),
            P(),
            P(None, "mp"),
            P(None, "mp"),
            P(None, "mp"),
            P("mp", None),
            P(None, "mp"),
            P(None, "mp"),
            P("mp", None),
            P(),
        ),
        out_specs=(P("mp", "round", None), P()),
        check_vma=False,
    )
```
